128 devices in a mesh: grp: 8 (over z_lo, y), inner: 16 (over x, z_hi, core).
Axes of the slice: x: 4, y: 4, z: 4 (z_hi: 2, z_lo: 2; z = z_hi * 2 + z_lo), core: 2. Of those that a mesh axis runs over, the one named last changes fastest.
Arguments:
- tokens: bfloat16 [2048, 8192], P('inner', 'grp'), may hold values from -170 to 170
- norm_gain: bfloat16 [8192], P('grp'), may hold values from 0.5 to 2
- gate_up_weight: bfloat16 [2, 8192, 28672], P(None, 'grp', 'inner'), may hold values from -0.0625 to 0.0625
- down_weight: bfloat16 [28672, 8192], P('inner', 'grp'), may hold values from -0.03125 to 0.03125
- student_in: bfloat16 [2048, 1024], P('grp'), may hold values from -6 to 6
- student_proj: bfloat16 [1024, 8192], P(None, 'inner'), may hold values from -0.1875 to 0.1875
Outputs:
- teacher_out: bfloat16 [2048, 8192], P('inner', 'grp')
- grad_student: float32 [2048, 1024], P('grp')
- grad_proj: float32 [1024, 8192], P(None, 'inner')
The draws below stay inside these ranges and needn't reach their ends.
All inputs are finite; a program needn't handle non-finite values.
Results may differ from the reference program's by a relative error of at most 0.025.
Values may be sent and summed in bfloat16 or wider, within the bound.
A program may use at most 128 MiB of HBM per device.

```python
import math
import jax
import jax.numpy as jnp
from jax import lax

D = 8192
FF = 28672
SD = 1024
ROWS = 2048
N_GRP = 8


def draw_tokens(key, part):
    subkeys = jax.random.split(jax.random.fold_in(key, 11), 3)
    column_rise = 3.0 ** (jnp.arange(D, dtype=jnp.float32) / D) * jax.random.uniform(subkeys[1], (D,), jnp.float32, 0.7, 1.4)
    row_scale = jnp.exp(jax.random.uniform(subkeys[2], (ROWS, 1), jnp.float32, 0.0, math.log(10.0)))
    entries = jnp.clip(jax.random.normal(subkeys[0], (ROWS, D), jnp.float32), -4.0, 4.0)
    return (entries * column_rise[None, :] * row_scale).astype(jnp.bfloat16)


def steps_of(stream_key, extent, shards, smallest, top_value):
    factor_of, own = 1.0, jax.random.fold_in(stream_key, 6)
    for axis_at, shards_of in shards:
        heights = jnp.exp(jax.random.uniform(jax.random.fold_in(own, axis_at), (shards_of,), jnp.float32, smallest / len(shards), top_value / len(shards)))
        factor_of = factor_of * jnp.repeat(heights, extent[axis_at] // shards_of).reshape([-1 if axis == axis_at else 1 for axis in range(len(extent))])
    return factor_of


def noise(key, extent, width, reach, cuts=(), held_as=jnp.bfloat16):
    level = steps_of(key, extent, cuts, -0.22, 0.18) if cuts else 1.0
    values = jax.random.normal(key, extent, jnp.float32) * width * level
    return jnp.minimum(jnp.maximum(values, -reach), reach).astype(held_as)


def setup_inputs(seed: int = 0) -> dict:
    arg_keys = jax.random.split(jax.random.key(seed), 7)
    tokens = draw_tokens(jax.random.fold_in(arg_keys[6], 71), 0)
    norm_gain = jnp.clip(jnp.exp(math.log(2.0) - 1.3862944 * jax.random.uniform(arg_keys[1], (D,), jnp.float32) ** steps_of(arg_keys[1], (D,), ((0, 8),), -0.2, 0.2)), 0.5, 2.0).astype(jnp.bfloat16)
    gate_up_weight = noise(arg_keys[2], (2, D, FF), D ** -0.5, 0.0625, ((1, 8), (2, 16)))
    down_weight = noise(arg_keys[3], (FF, D), FF ** -0.5, 0.03125, ((0, 16), (1, 8)))
    student_in = noise(arg_keys[4], (ROWS, SD), 1.0, 6.0, ((0, 8),))
    student_proj = noise(arg_keys[5], (SD, D), SD ** -0.5, 0.1875, ((1, 16),))
    return dict(tokens=tokens, norm_gain=norm_gain, gate_up_weight=gate_up_weight, down_weight=down_weight, student_in=student_in, student_proj=student_proj)


def reference(tokens, norm_gain, gate_up_weight, down_weight, student_in, student_proj):
    values = tokens.astype(jnp.float32)
    mean_square = lax.optimization_barrier(jnp.mean(values * values, axis=1, keepdims=True))
    normed = (values * lax.rsqrt(mean_square + 1e-05) * norm_gain.astype(jnp.float32)[None, :]).astype(jnp.bfloat16)
    block_width = D // N_GRP
    gate_sum = jnp.zeros((ROWS, FF), jnp.float32)
    up_sum = jnp.zeros((ROWS, FF), jnp.float32)
    for block_index in range(N_GRP):
        lower = block_index * block_width
        piece = normed[:, lower:lower + block_width]
        gate_term = jnp.dot(piece, gate_up_weight[0, lower:lower + block_width, :], preferred_element_type=jnp.float32)
        up_term = jnp.dot(piece, gate_up_weight[1, lower:lower + block_width, :], preferred_element_type=jnp.float32)
        gate_sum = gate_sum + gate_term.astype(jnp.bfloat16).astype(jnp.float32)
        up_sum = up_sum + up_term.astype(jnp.bfloat16).astype(jnp.float32)
    hidden = (jax.nn.silu(gate_sum) * up_sum).astype(jnp.bfloat16)
    teacher_out = jnp.dot(hidden, down_weight, preferred_element_type=jnp.float32).astype(jnp.bfloat16)
    predicted = jnp.tanh(jnp.dot(student_in, student_proj, preferred_element_type=jnp.float32))
    mismatch = predicted - teacher_out.astype(jnp.float32)
    pre_grad = (mismatch * (1.0 - predicted * predicted)).astype(jnp.bfloat16)
    grad_student = jnp.dot(pre_grad, student_proj.T, preferred_element_type=jnp.float32)
    grad_proj = jnp.dot(student_in.T, pre_grad, preferred_element_type=jnp.float32)
    return (teacher_out, grad_student, grad_proj)
```

```python
import jax
import jax.numpy as jnp
from jax import lax
from jax.experimental import pallas as pl
from jax.experimental.pallas import tpu as pltpu
from jax.sharding import PartitionSpec as P

D = 8192
KB = 1024
FB = 1792
F2 = 2 * FB
SD = 1024
SC = 512
C = 8
MC = 256
HR = 32
NS = 3
GROUPS = ((0, 1), (1, 1), (2, 2), (4, 4))
FAR = 4
f32, bf16 = jnp.float32, jnp.bfloat16
MESH = pl.DeviceIdType.MESH


def kernel(
    tok_ref, gain_ref, w_hbm, wd_hbm, sin_hbm, proj_hbm,
    teach_ref, gstu_ref, gproj_ref,
    w, wd, proj, xb, sall, ssq, ssqr,
    gs, ra, rb, rz, hb, ps, rc, px, rx, pz, rzh, th, tgt, pgs, it, rr, fin, rf,
    lsem, ssq_s, ssq_r, s1_s, s1_r, t1_s, t1_r, t2_s, t2_r, t3_s, t3_r,
    rs_s, rs_r, hz_s, hz_r, c_s, c_r, x_s, x_r, zh_s, zh_r, p_s, p_r, a_s, a_r, b_s, b_r,
):
    g = lax.axis_index("grp")
    i = lax.axis_index("inner")
    z, y = g // 4, g % 4
    x, core, q = i // 4, i % 2, i // 2
    yp, ym, yd = (y + 1) % 4, (y + 3) % 4, (y + 2) % 4
    gp, gm = z * 4 + yp, z * 4 + ym
    gz = (1 - z) * 4 + y
    oz = 1 - z
    zh = q % 2
    izh = x * 4 + (1 - zh) * 2 + core
    icore = x * 4 + zh * 2 + (1 - core)
    pos = core * 8 + q
    me_far = g == q

    def rcopy(src, dst, ss, rs, dg, di):
        return pltpu.make_async_remote_copy(
            src_ref=src, dst_ref=dst, send_sem=ss, recv_sem=rs,
            device_id=(dg, di), device_id_type=MESH,
        )

    load_w = pltpu.make_async_copy(w_hbm, w, lsem.at[0])
    load_wd = pltpu.make_async_copy(wd_hbm, wd, lsem.at[1])
    load_proj = pltpu.make_async_copy(proj_hbm, proj, lsem.at[2])
    rows16 = pl.ds(pl.multiple_of(pos * 16, 16), 16)
    my16 = pl.ds(pl.multiple_of(g * 16, 16), 16)
    load_sin = pltpu.make_async_copy(
        sin_hbm.at[rows16], sall.at[core, q, my16], lsem.at[3]
    )
    load_w.start()
    load_wd.start()
    load_proj.start()
    load_sin.start()

    barrier = pltpu.get_barrier_semaphore()

    def greet_grp(d, _):
        pl.semaphore_signal(barrier, inc=1, device_id=((g + d) % 8, i), device_id_type=MESH)
        return 0

    def greet_inner(d, _):
        pl.semaphore_signal(barrier, inc=1, device_id=(g, (i + d) % 16), device_id_type=MESH)
        return 0

    def greet_far(j, _):
        @pl.when(jnp.logical_not(me_far & (j == i)))
        def _():
            pl.semaphore_signal(barrier, inc=1, device_id=(q, j), device_id_type=MESH)
        return 0

    lax.fori_loop(1, 8, greet_grp, 0)
    lax.fori_loop(1, 16, greet_inner, 0)
    lax.fori_loop(0, 16, greet_far, 0)

    values = tok_ref[...].astype(f32)
    total = jnp.sum(values * values, axis=1, keepdims=True)
    ssq[...] = jnp.broadcast_to(total, (128, 128)).T[0:8]

    pl.semaphore_wait(barrier, jnp.where(me_far & (i // 2 == g), 37, 38))

    def ssq_copy(d):
        return rcopy(ssq, ssqr.at[7 - d], ssq_s.at[d - 1], ssq_r, (g + d) % 8, i)

    def s1_copy(d):
        return rcopy(
            sin_hbm.at[rows16], sall.at[core, q, my16], s1_s.at[d - 1], s1_r, (g + d) % 8, i
        )

    for d in range(1, 8):
        ssq_copy(d).start()
    pltpu.make_async_copy(ssqr, ssqr, ssq_r).wait()
    line = ssq[0:1, :]
    for d in range(7):
        line = line + ssqr[d, 0:1, :]
    column = jnp.broadcast_to(line, (128, 128)).T[:, 0:1]
    inverse = lax.rsqrt(column / D + 1e-05)
    normed = (values * inverse * gain_ref[...].astype(f32)).astype(bf16)
    xb[:, core, q] = normed.reshape(8, 16, KB)

    x2 = pl.ds(pl.multiple_of(x * 2, 2), 2)

    def t1(k):
        if k == FAR:
            ref = sall.at[core, q]
        else:
            ref = xb.at[pl.ds(GROUPS[k][0], GROUPS[k][1]), core, q]
        return rcopy(ref, ref, t1_s.at[k], t1_r.at[k], g, izh)

    def t2(k, d):
        if k == FAR:
            ref = sall.at[core, x2]
        else:
            ref = xb.at[pl.ds(GROUPS[k][0], GROUPS[k][1]), core, x2]
        return rcopy(ref, ref, t2_s.at[k, d - 1], t2_r.at[k, d - 1], g, (i + 4 * d) % 16)

    def t3(k):
        if k == FAR:
            ref = sall.at[core]
        else:
            ref = xb.at[pl.ds(GROUPS[k][0], GROUPS[k][1]), core]
        return rcopy(ref, ref, t3_s.at[k], t3_r.at[k], g, icore)

    def start_t2(k):
        t1(k).wait_recv()
        for d in (2, 1, 3):
            t2(k, d).start()

    def start_t3(k):
        for d in (1, 3, 2):
            t2(k, d).wait_recv()
        t3(k).start()

    for k in range(4):
        t1(k).start()
    load_sin.wait()
    for d in range(1, 8):
        s1_copy(d).start()
    for k in range(4):
        start_t2(k)
    start_t3(0)
    load_w.wait()

    def slot(c):
        return lax.rem(c, NS)

    def a_p(c):
        s = slot(c)
        return rcopy(gs.at[s, yd, 0], ra.at[s, 0], rs_s.at[0, s], rs_r.at[0, s], gp, i)

    def a_m(c):
        s = slot(c)
        return rcopy(gs.at[s, yd, 1], ra.at[s, 1], rs_s.at[1, s], rs_r.at[1, s], gm, i)

    def b1_p(c):
        s = slot(c)
        return rcopy(gs.at[s, yp, 1], rb.at[s, 0, 1], rs_s.at[2, s], rs_r.at[2, s], gp, i)

    def b1_m(c):
        s = slot(c)
        return rcopy(gs.at[s, ym, 0], rb.at[s, 1, 0], rs_s.at[3, s], rs_r.at[3, s], gm, i)

    def b2_p(c):
        s = slot(c)
        return rcopy(gs.at[s, yp, 0], rb.at[s, 0, 0], rs_s.at[4, s], rs_r.at[4, s], gp, i)

    def b2_m(c):
        s = slot(c)
        return rcopy(gs.at[s, ym, 1], rb.at[s, 1, 1], rs_s.at[5, s], rs_r.at[5, s], gm, i)

    def zc(c):
        s = slot(c)
        return rcopy(gs.at[s, y, oz], rz.at[s], rs_s.at[6, s], rs_r.at[6, s], gz, i)

    def e_p(c):
        s = slot(c)
        ref = hb.at[s, y, z]
        return rcopy(ref, ref, hz_s.at[0, s], hz_r.at[0, s], gp, i)

    def e_m(c):
        s = slot(c)
        ref = hb.at[s, y, z]
        return rcopy(ref, ref, hz_s.at[1, s], hz_r.at[1, s], gm, i)

    def f_p(c):
        s = slot(c)
        ref = hb.at[s, ym, z, pl.ds(0, 16)]
        return rcopy(ref, ref, hz_s.at[2, s], hz_r.at[2, s], gp, i)

    def f_m(c):
        s = slot(c)
        ref = hb.at[s, yp, z, pl.ds(16, 16)]
        return rcopy(ref, ref, hz_s.at[3, s], hz_r.at[3, s], gm, i)

    def ez(c, block, n):
        s = slot(c)
        ref = hb.at[s, block, z]
        return rcopy(ref, ref, hz_s.at[4 + n, s], hz_r.at[4 + n, s], gz, i)

    def wait_grp_sends(c):
        for copy in (a_p, a_m, b1_p, b1_m, b2_p, b2_m, zc, e_p, e_m, f_p, f_m):
            copy(c).wait_send()
        for n, block in enumerate((y, ym, yp, yd)):
            ez(c, block, n).wait_send()

    def stage_g(c):
        s = slot(c)
        rows = xb.at[c].reshape(MC, KB)
        for k in range(2):
            @pl.loop(0, 7)
            def _(n):
                cols = pl.ds(pl.multiple_of(n * 256, 256), 256)
                out = jnp.dot(rows[...], w[k, :, cols], preferred_element_type=f32)
                gs[s, :, :, :, pl.ds(pl.multiple_of(k * FB + n * 256, 256), 256)] = (
                    out.astype(bf16).reshape(4, 2, HR, 256)
                )
        a_p(c).start()
        a_m(c).start()
        b1_p(c).start()
        b1_m(c).start()

    def stage_r1(c):
        s = slot(c)
        a_p(c).wait_recv()
        gs[s, yp, 0] = (gs[s, yp, 0].astype(f32) + ra[s, 0].astype(f32)).astype(bf16)
        b2_p(c).start()
        a_m(c).wait_recv()
        gs[s, ym, 1] = (gs[s, ym, 1].astype(f32) + ra[s, 1].astype(f32)).astype(bf16)
        b2_m(c).start()

    def stage_r2(c):
        s = slot(c)
        for copy in (b1_p, b1_m, b2_p, b2_m):
            copy(c).wait_recv()
        gs[s, y, oz] = (
            gs[s, y, oz].astype(f32) + rb[s, 0, oz].astype(f32) + rb[s, 1, oz].astype(f32)
        ).astype(bf16)
        zc(c).start()

    def stage_r3(c):
        s = slot(c)
        zc(c).wait_recv()

        def part(cols):
            return (
                gs[s, y, z, :, cols].astype(f32) + rb[s, 0, z, :, cols].astype(f32)
                + rb[s, 1, z, :, cols].astype(f32) + rz[s, :, cols].astype(f32)
            )

        for n in range(7):
            gate = part(pl.ds(n * 256, 256))
            up = part(pl.ds(FB + n * 256, 256))
            hb[s, y, z, :, pl.ds(n * 256, 256)] = (gate / (1.0 + jnp.exp(-gate)) * up).astype(bf16)
        e_p(c).start()
        e_m(c).start()
        ez(c, y, 0).start()

    def stage_r4(c):
        e_p(c).wait_recv()
        f_p(c).start()
        e_m(c).wait_recv()
        f_m(c).start()
        ez(c, ym, 1).start()
        ez(c, yp, 2).start()

    def stage_r5(c):
        f_p(c).wait_recv()
        f_m(c).wait_recv()
        ez(c, yd, 3).start()

    def cc(c):
        s = lax.rem(c, 2)
        return rcopy(ps.at[s, 1 - core], rc.at[c], c_s.at[s], c_r.at[c], g, icore)

    def xc(c, d):
        s = lax.rem(c, 2)
        return rcopy(
            px.at[s, (x + d) % 4], rx.at[c, d - 1], x_s.at[d - 1, s], x_r.at[d - 1, c],
            g, (i + 4 * d) % 16,
        )

    def zhc(c):
        s = lax.rem(c, 2)
        return rcopy(pz.at[s], rzh.at[c], zh_s.at[s], zh_r.at[c], g, izh)

    def stage_dn(c):
        s, s2 = slot(c), lax.rem(c, 2)
        for n, block in enumerate((y, ym, yp, yd)):
            ez(c, block, n).wait_recv()
        rows = hb.at[s].reshape(MC, FB)

        @pl.loop(0, 4)
        def _(n):
            cols = pl.ds(pl.multiple_of(n * 256, 256), 256)
            out = jnp.dot(rows[...], wd[:, cols], preferred_element_type=f32)
            ps[s2, :, :, cols] = out.astype(bf16).reshape(2, 128, 256)

        cc(c).start()

    def stage_u1(c):
        s2 = lax.rem(c, 2)
        cc(c).wait_recv()
        px[s2] = (ps[s2, core].astype(f32) + rc[c].astype(f32)).astype(bf16).reshape(4, 2, 16, KB)
        for d in (2, 1, 3):
            xc(c, d).start()
        cc(c).wait_send()

    def sum_x(c, half):
        s2 = lax.rem(c, 2)
        out = px[s2, x, half].astype(f32)
        for d in range(3):
            out = out + rx[c, d, half].astype(f32)
        return out

    def stage_u2(c):
        for d in (1, 3, 2):
            xc(c, d).wait_recv()
        pz[lax.rem(c, 2)] = sum_x(c, 1 - zh).astype(bf16)
        zhc(c).start()

    def far_copy(c, j):
        return rcopy(
            th.at[c, j % 2], tgt.at[c, pos], p_s.at[j], p_r.at[c], j // 2, 2 * g + j % 2
        )

    def far_self(c):
        return pltpu.make_async_copy(th.at[c, core], tgt.at[c, pos], p_r.at[c])

    def far_is_self(j):
        return me_far & (j == 2 * g + core)

    def stage_u3(c):
        zhc(c).wait_recv()
        out = (sum_x(c, zh) + rzh[c].astype(f32)).astype(bf16)
        teach_ref[c] = out
        th[c, 0] = out[:, :SC]
        th[c, 1] = out[:, SC:]

        def send(j, _):
            @pl.when(far_is_self(j))
            def _():
                far_self(c).start()

            @pl.when(jnp.logical_not(far_is_self(j)))
            def _():
                far_copy(c, j).start()
            return 0

        lax.fori_loop(0, 16, send, 0)
        for d in (1, 2, 3):
            xc(c, d).wait_send()
        zhc(c).wait_send()

    def stage_v(c):
        rows = jnp.concatenate([sall[0, c], sall[1, c]], axis=0)
        predicted = jnp.tanh(jnp.dot(rows, proj[...], preferred_element_type=f32))
        pltpu.make_async_copy(tgt.at[c], tgt.at[c], p_r.at[c]).wait()
        target = tgt[c].reshape(MC, SC).astype(f32)
        pre = ((predicted - target) * (1.0 - predicted * predicted)).astype(bf16)
        pgs[c] = pre.reshape(2, 8, 16, SC)
        for n in range(4):
            cols = slice(n * 256, n * 256 + 256)
            gproj_ref[cols, :] += lax.dot_general(
                rows[:, cols], pre, (((0,), (0,)), ((), ())), preferred_element_type=f32
            )

        def done(j, _):
            @pl.when(jnp.logical_not(far_is_self(j)))
            def _():
                far_copy(c, j).wait_send()
            return 0

        lax.fori_loop(0, 16, done, 0)

    gproj_ref[...] = jnp.zeros_like(gproj_ref)

    def tick(t, _):
        def run(stage, back):
            c = t - back

            @pl.when((c >= 0) & (c < C))
            def _():
                stage(c)

        run(wait_grp_sends, 3)
        for k in range(4):
            @pl.when(t == GROUPS[k][0])
            def _():
                t3(k).wait_recv()
        run(stage_g, 0)
        run(stage_u3, 3)
        run(stage_r2, 1)
        run(stage_r5, 2)

        @pl.when(t == 2)
        def _():
            load_wd.wait()

        run(stage_dn, 2)
        run(stage_r1, 0)
        run(stage_u1, 2)
        run(stage_r3, 1)

        @pl.when(t == 3)
        def _():
            load_proj.wait()
            t3(FAR).wait_recv()

        run(stage_v, 3)
        run(stage_u2, 2)
        run(stage_r4, 1)

        @pl.when(t == 0)
        def _():
            start_t3(1)
            pltpu.make_async_copy(
                sall.at[core, q, pl.ds(0, 112)], sall.at[core, q, pl.ds(0, 112)], s1_r
            ).wait()
            t1(FAR).start()

        @pl.when(t == 1)
        def _():
            start_t3(2)
            start_t2(FAR)

        @pl.when(t == 2)
        def _():
            start_t3(3)
            start_t3(FAR)
        return 0

    lax.fori_loop(0, C + 3, tick, 0)

    own = jnp.concatenate(
        [pgs[c, b, g] for b in range(2) for c in range(C)], axis=0
    )
    for n in range(4):
        rows = slice(n * 256, n * 256 + 256)
        it[:, :, rows] = lax.dot_general(
            own, proj[rows, :], (((1,), (1,)), ((), ())), preferred_element_type=f32
        ).astype(bf16).reshape(16, 16, 256)

    def a_copy(d):
        return rcopy(it.at[(i + d) % 16], rr.at[15 - d], a_s.at[d - 1], a_r, g, (i + d) % 16)

    def b_copy(d):
        return rcopy(fin, rf.at[i], b_s.at[d - 1], b_r, g, (i + d) % 16)

    def each(copy, what):
        def body(d, _):
            what(copy(d))
            return 0
        lax.fori_loop(1, 16, body, 0)

    each(a_copy, lambda copy: copy.start())
    pltpu.make_async_copy(rr, rr, a_r).wait()
    out = it[i].astype(f32)
    for d in range(15):
        out = out + rr[d].astype(f32)
    fin[...] = out.astype(bf16)
    each(b_copy, lambda copy: copy.start())
    pltpu.make_async_copy(rf.at[pl.ds(0, 15)], rf.at[pl.ds(0, 15)], b_r).wait()
    rf[i] = fin[...]
    gstu_ref[...] = rf[...].reshape(256, SD).astype(f32)

    for d in range(1, 8):
        ssq_copy(d).wait_send()
        s1_copy(d).wait_send()
    for k in range(5):
        t1(k).wait_send()
        for d in range(1, 4):
            t2(k, d).wait_send()
        t3(k).wait_send()
    each(a_copy, lambda copy: copy.wait_send())
    each(b_copy, lambda copy: copy.wait_send())


def shards(tokens, norm_gain, gate_up_weight, down_weight, student_in, student_proj):
    vmem = pl.BlockSpec(memory_space=pltpu.VMEM)
    hbm = pl.BlockSpec(memory_space=pl.ANY)
    dma = pltpu.SemaphoreType.DMA
    teacher, grad_student, grad_proj = pl.pallas_call(
        kernel,
        out_shape=(
            jax.ShapeDtypeStruct((C, 16, KB), bf16),
            jax.ShapeDtypeStruct((256, SD), f32),
            jax.ShapeDtypeStruct((SD, SC), f32),
        ),
        in_specs=[vmem, vmem, hbm, hbm, hbm, hbm],
        out_specs=(vmem, vmem, vmem),
        scratch_shapes=[
            pltpu.VMEM((2, KB, FB), bf16),
            pltpu.VMEM((FB, KB), bf16),
            pltpu.VMEM((SD, SC), bf16),
            pltpu.VMEM((C, 2, 8, 16, KB), bf16),
            pltpu.VMEM((2, 8, 128, SD), bf16),
            pltpu.VMEM((8, 128), f32),
            pltpu.VMEM((7, 8, 128), f32),
            pltpu.VMEM((NS, 4, 2, HR, F2), bf16),
            pltpu.VMEM((NS, 2, HR, F2), bf16),
            pltpu.VMEM((NS, 2, 2, HR, F2), bf16),
            pltpu.VMEM((NS, HR, F2), bf16),
            pltpu.VMEM((NS, 4, 2, HR, FB), bf16),
            pltpu.VMEM((2, 2, 128, KB), bf16),
            pltpu.VMEM((C, 128, KB), bf16),
            pltpu.VMEM((2, 4, 2, 16, KB), bf16),
            pltpu.VMEM((C, 3, 2, 16, KB), bf16),
            pltpu.VMEM((2, 16, KB), bf16),
            pltpu.VMEM((C, 16, KB), bf16),
            pltpu.VMEM((C, 2, 16, SC), bf16),
            pltpu.VMEM((C, 16, 16, SC), bf16),
            pltpu.VMEM((C, 2, 8, 16, SC), bf16),
            pltpu.VMEM((16, 16, SD), bf16),
            pltpu.VMEM((15, 16, SD), bf16),
            pltpu.VMEM((16, SD), bf16),
            pltpu.VMEM((16, 16, SD), bf16),
            dma((4,)),
            dma((7,)), dma(()),
            dma((7,)), dma(()),
            dma((5,)), dma((5,)),
            dma((5, 3)), dma((5, 3)),
            dma((5,)), dma((5,)),
            dma((7, NS)), dma((7, NS)),
            dma((8, NS)), dma((8, NS)),
            dma((2,)), dma((C,)),
            dma((3, 2)), dma((3, C)),
            dma((2,)), dma((C,)),
            dma((16,)), dma((C,)),
            dma((15,)), dma(()),
            dma((15,)), dma(()),
        ],
        compiler_params=pltpu.CompilerParams(
            collective_id=0, has_side_effects=True, vmem_limit_bytes=62 * 1024 * 1024
        ),
    )(tokens, norm_gain.reshape(1, KB), gate_up_weight, down_weight, student_in, student_proj)
    return teacher.reshape(128, KB), grad_student, grad_proj


def solution(mesh):
    return jax.shard_map(
        shards,
        mesh=mesh,
        in_specs=(
            P("inner", "grp"),
            P("grp"),
            P(None, "grp", "inner"),
            P("inner", "grp"),
            P("grp", None),
            P(None, "inner"),
        ),
        out_specs=(P("inner", "grp"), P("grp", None), P(None, "inner")),
        check_vma=False,
    )
```

```python
import jax
import jax.numpy as jnp
from jax import lax
from jax.experimental import pallas as pl
from jax.experimental.pallas import tpu as pltpu
from jax.sharding import PartitionSpec as P

D = 8192
KB = 1024
FB = 1792
F2 = 2 * FB
SD = 1024
SC = 512
C = 8
MC = 256
HR = 32
NS = 4
GROUPS = ((0, 1), (1, 1), (2, 2), (4, 4))
FAR = 4
f32, bf16 = jnp.float32, jnp.bfloat16
MESH = pl.DeviceIdType.MESH


def kernel(
    tok_ref, gain_ref, w_hbm, wd_hbm, sin_hbm, proj_hbm,
    teach_ref, gstu_ref, gproj_ref,
    w, wd, proj, sin, pred, xb, sall, ssq, ssqr, inv_own, inv_line, inv,
    gs, ra, rb, rz, hb, ps, rc, px, rx, pz, rzh, th, tgt, pg, gproj, it, rr, rf,
    lsem, ssq_s, ssq_r, inv_s, inv_r, s1_s, s1_r, t1_s, t1_r, t2_s, t2_r, t3_s, t3_r,
    rs_s, rs_r, hz_s, hz_r, c_s, c_r, x_s, x_r, zh_s, zh_r, p_s, p_r,
    py_s, py_r, pz_s, pz_r, a_s, a_r, b_s, b_r,
):
    g = lax.axis_index("grp")
    i = lax.axis_index("inner")
    z, y = g // 4, g % 4
    x, core, q = i // 4, i % 2, i // 2
    yp, ym, yd = (y + 1) % 4, (y + 3) % 4, (y + 2) % 4
    gp, gm = z * 4 + yp, z * 4 + ym
    gz = (1 - z) * 4 + y
    oz = 1 - z
    zh = q % 2
    izh = x * 4 + (1 - zh) * 2 + core
    icore = x * 4 + zh * 2 + (1 - core)
    pos = core * 8 + q
    me_far = g == q

    def rcopy(src, dst, ss, rs, dg, di):
        return pltpu.make_async_remote_copy(
            src_ref=src, dst_ref=dst, send_sem=ss, recv_sem=rs,
            device_id=(dg, di), device_id_type=MESH,
        )

    load_w = pltpu.make_async_copy(w_hbm, w, lsem.at[0])
    load_wd = pltpu.make_async_copy(wd_hbm, wd, lsem.at[1])
    load_proj = pltpu.make_async_copy(proj_hbm, proj, lsem.at[2])
    rows16 = pl.ds(pl.multiple_of(pos * 16, 16), 16)
    my16 = pl.ds(pl.multiple_of(g * 16, 16), 16)
    load_sin = pltpu.make_async_copy(sin_hbm, sin, lsem.at[3])
    load_w.start()
    load_wd.start()
    load_proj.start()
    load_sin.start()

    barrier = pltpu.get_barrier_semaphore()

    def greet_grp(d, _):
        pl.semaphore_signal(barrier, inc=1, device_id=((g + d) % 8, i), device_id_type=MESH)
        return 0

    def greet_inner(d, _):
        pl.semaphore_signal(barrier, inc=1, device_id=(g, (i + d) % 16), device_id_type=MESH)
        return 0

    lax.fori_loop(1, 8, greet_grp, 0)
    lax.fori_loop(1, 16, greet_inner, 0)
    for h in range(2):
        @pl.when(jnp.logical_not(me_far & (core == h)))
        def _():
            pl.semaphore_signal(barrier, inc=1, device_id=(q, 2 * g + h), device_id_type=MESH)

    values = tok_ref[...].astype(f32)
    total = jnp.sum(values * values, axis=1, keepdims=True)
    ssq[...] = jnp.broadcast_to(total, (128, 128)).T[0:8]

    xb[:, core, q] = (values * gain_ref[...].astype(f32)).astype(bf16).reshape(8, 16, KB)
    pl.semaphore_wait(barrier, jnp.where(me_far, 23, 24))

    def ssq_copy(d):
        return rcopy(ssq, ssqr.at[7 - d], ssq_s.at[d - 1], ssq_r, (g + d) % 8, i)

    def s1_copy(d):
        return rcopy(
            sin.at[rows16], sall.at[core, q, my16], s1_s.at[d - 1], s1_r, (g + d) % 8, i
        )

    teller = g == ((q // 2) % 2) * 4 + core * 2 + q // 4

    def inv_copy(d):
        return rcopy(inv_own, inv_line.at[q % 2], inv_s.at[d - 1], inv_r.at[q % 2], g, (i + d) % 16)

    def scales():
        pltpu.make_async_copy(ssqr, ssqr, ssq_r).wait()
        line = ssq[...]
        for d in range(7):
            line = line + ssqr[d]
        inv_own[...] = lax.rsqrt(line / D + 1e-05)

        @pl.when(teller)
        def _():
            for d in range(1, 16):
                inv_copy(d).start()

    def scale_columns():
        for k in range(2):
            mine = teller & (q % 2 == k)

            @pl.when(mine)
            def _():
                inv_line[k] = inv_own[...]

            @pl.when(jnp.logical_not(mine))
            def _():
                pltpu.make_async_copy(inv_line.at[k], inv_line.at[k], inv_r.at[k]).wait()

            inv[k] = jnp.broadcast_to(inv_line[k, 0:1], (128, 128)).T.reshape(C, 16, 128)

    x2 = pl.ds(pl.multiple_of(x * 2, 2), 2)

    def t1(k):
        if k == FAR:
            ref = sall.at[core, q]
        else:
            ref = xb.at[pl.ds(GROUPS[k][0], GROUPS[k][1]), core, q]
        return rcopy(ref, ref, t1_s.at[k], t1_r.at[k], g, izh)

    def t2(k, d):
        if k == FAR:
            ref = sall.at[core, x2]
        else:
            ref = xb.at[pl.ds(GROUPS[k][0], GROUPS[k][1]), core, x2]
        return rcopy(ref, ref, t2_s.at[k, d - 1], t2_r.at[k, d - 1], g, (i + 4 * d) % 16)

    def t3(k):
        if k == FAR:
            ref = sall.at[core]
        else:
            ref = xb.at[pl.ds(GROUPS[k][0], GROUPS[k][1]), core]
        return rcopy(ref, ref, t3_s.at[k], t3_r.at[k], g, icore)

    def start_t2(k):
        t1(k).wait_recv()
        for d in (2, 1, 3):
            t2(k, d).start()

    def start_t3(k):
        for d in (1, 3, 2):
            t2(k, d).wait_recv()
        t3(k).start()

    for k in range(4):
        t1(k).start()
    for d in range(1, 8):
        ssq_copy(d).start()
    start_t2(0)
    start_t3(0)
    scales()
    for k in range(1, 4):
        start_t2(k)
    load_sin.wait()
    sall[core, q, my16] = sin[rows16]
    for d in range(1, 8):
        s1_copy(d).start()
    load_w.wait()

    def slot(c):
        return lax.rem(c, NS)

    def a_p(c):
        s = slot(c)
        return rcopy(gs.at[s, yd, 0], ra.at[s, 0], rs_s.at[0, s], rs_r.at[0, s], gp, i)

    def a_m(c):
        s = slot(c)
        return rcopy(gs.at[s, yd, 1], ra.at[s, 1], rs_s.at[1, s], rs_r.at[1, s], gm, i)

    def b1_p(c):
        s = slot(c)
        return rcopy(gs.at[s, yp, 1], rb.at[s, 0, 1], rs_s.at[2, s], rs_r.at[2, s], gp, i)

    def b1_m(c):
        s = slot(c)
        return rcopy(gs.at[s, ym, 0], rb.at[s, 1, 0], rs_s.at[3, s], rs_r.at[3, s], gm, i)

    def b2_p(c):
        s = slot(c)
        return rcopy(gs.at[s, yp, 0], rb.at[s, 0, 0], rs_s.at[4, s], rs_r.at[4, s], gp, i)

    def b2_m(c):
        s = slot(c)
        return rcopy(gs.at[s, ym, 1], rb.at[s, 1, 1], rs_s.at[5, s], rs_r.at[5, s], gm, i)

    def zc(c):
        s = slot(c)
        return rcopy(gs.at[s, y, oz], rz.at[s], rs_s.at[6, s], rs_r.at[6, s], gz, i)

    def e_p(c):
        s = slot(c)
        ref = hb.at[s, y, z]
        return rcopy(ref, ref, hz_s.at[0, s], hz_r.at[0, s], gp, i)

    def e_m(c):
        s = slot(c)
        ref = hb.at[s, y, z]
        return rcopy(ref, ref, hz_s.at[1, s], hz_r.at[1, s], gm, i)

    def f_p(c):
        s = slot(c)
        ref = hb.at[s, ym, z, pl.ds(0, 16)]
        return rcopy(ref, ref, hz_s.at[2, s], hz_r.at[2, s], gp, i)

    def f_m(c):
        s = slot(c)
        ref = hb.at[s, yp, z, pl.ds(16, 16)]
        return rcopy(ref, ref, hz_s.at[3, s], hz_r.at[3, s], gm, i)

    def ez(c, block, n):
        s = slot(c)
        ref = hb.at[s, block, z]
        return rcopy(ref, ref, hz_s.at[4 + n, s], hz_r.at[4 + n, s], gz, i)

    def wait_grp_sends(c):
        for copy in (a_p, a_m, b1_p, b1_m, b2_p, b2_m, zc, e_p, e_m, f_p, f_m):
            copy(c).wait_send()
        for n, block in enumerate((y, ym, yp, yd)):
            ez(c, block, n).wait_send()

    def stage_g(c):
        s = slot(c)
        rows = xb.at[c].reshape(MC, KB)
        for k in range(2):
            @pl.loop(0, 7)
            def _(n):
                cols = pl.ds(pl.multiple_of(n * 256, 256), 256)
                out = jnp.dot(rows[...], w[k, :, cols], preferred_element_type=f32)
                gs[s, :, :, :, pl.ds(pl.multiple_of(k * FB + n * 256, 256), 256)] = (
                    out.astype(bf16).reshape(4, 2, HR, 256)
                )
        a_p(c).start()
        a_m(c).start()
        b1_p(c).start()
        b1_m(c).start()

    def stage_r1(c):
        s = slot(c)
        a_p(c).wait_recv()
        gs[s, yp, 0] = (gs[s, yp, 0].astype(f32) + ra[s, 0].astype(f32)).astype(bf16)
        b2_p(c).start()
        a_m(c).wait_recv()
        gs[s, ym, 1] = (gs[s, ym, 1].astype(f32) + ra[s, 1].astype(f32)).astype(bf16)
        b2_m(c).start()

    def stage_r2(c):
        s = slot(c)
        for copy in (b1_p, b1_m, b2_p, b2_m):
            copy(c).wait_recv()
        gs[s, y, oz] = (
            gs[s, y, oz].astype(f32) + rb[s, 0, oz].astype(f32) + rb[s, 1, oz].astype(f32)
        ).astype(bf16)
        zc(c).start()

    def stage_r3(c):
        s = slot(c)
        zc(c).wait_recv()

        def part(cols):
            return (
                gs[s, y, z, :, cols].astype(f32) + rb[s, 0, z, :, cols].astype(f32)
                + rb[s, 1, z, :, cols].astype(f32) + rz[s, :, cols].astype(f32)
            )

        scale = jnp.concatenate([inv[0, c][:, 0:1], inv[1, c][:, 0:1]], axis=0)
        for n in range(7):
            gate = part(pl.ds(n * 256, 256)) * scale
            up = part(pl.ds(FB + n * 256, 256)) * scale
            hb[s, y, z, :, pl.ds(n * 256, 256)] = (gate / (1.0 + jnp.exp(-gate)) * up).astype(bf16)
        e_p(c).start()
        e_m(c).start()
        ez(c, y, 0).start()

    def stage_r4(c):
        e_p(c).wait_recv()
        f_p(c).start()
        e_m(c).wait_recv()
        f_m(c).start()
        ez(c, ym, 1).start()
        ez(c, yp, 2).start()

    def stage_r5(c):
        f_p(c).wait_recv()
        f_m(c).wait_recv()
        ez(c, yd, 3).start()

    def cc(c):
        s = lax.rem(c, 2)
        return rcopy(ps.at[s, 1 - core], rc.at[c], c_s.at[s], c_r.at[c], g, icore)

    def xc(c, d):
        s = lax.rem(c, 2)
        return rcopy(
            px.at[s, (x + d) % 4], rx.at[c, d - 1], x_s.at[d - 1, s], x_r.at[d - 1, c],
            g, (i + 4 * d) % 16,
        )

    def zhc(c):
        s = lax.rem(c, 2)
        return rcopy(pz.at[s], rzh.at[c], zh_s.at[s], zh_r.at[c], g, izh)

    def stage_dn(c):
        s, s2 = slot(c), lax.rem(c, 2)
        for n, block in enumerate((y, ym, yp, yd)):
            ez(c, block, n).wait_recv()
        rows = hb.at[s].reshape(MC, FB)

        @pl.loop(0, 4)
        def _(n):
            cols = pl.ds(pl.multiple_of(n * 256, 256), 256)
            out = jnp.dot(rows[...], wd[:, cols], preferred_element_type=f32)
            ps[s2, :, :, cols] = out.astype(bf16).reshape(2, 128, 256)

        cc(c).start()

    def stage_u1(c):
        s2 = lax.rem(c, 2)
        cc(c).wait_recv()
        px[s2] = (ps[s2, core].astype(f32) + rc[c].astype(f32)).astype(bf16).reshape(4, 2, 16, KB)
        for d in (2, 1, 3):
            xc(c, d).start()
        cc(c).wait_send()

    def sum_x(c, half):
        s2 = lax.rem(c, 2)
        out = px[s2, x, half].astype(f32)
        for d in range(3):
            out = out + rx[c, d, half].astype(f32)
        return out

    def stage_u2(c):
        for d in (1, 3, 2):
            xc(c, d).wait_recv()
        pz[lax.rem(c, 2)] = sum_x(c, 1 - zh).astype(bf16)
        zhc(c).start()

    def far_copy(c, h):
        return rcopy(th.at[c, h], tgt.at[c, core], p_s.at[h], p_r.at[c], q, 2 * g + h)

    def far(c, h, begin):
        own = me_far & (core == h)

        @pl.when(jnp.logical_not(own))
        def _():
            if begin:
                far_copy(c, h).start()
            else:
                far_copy(c, h).wait_send()

        if begin:
            @pl.when(own)
            def _():
                pltpu.make_async_copy(th.at[c, h], tgt.at[c, core], p_r.at[c]).start()

    def stage_u3(c):
        zhc(c).wait_recv()
        out = (sum_x(c, zh) + rzh[c].astype(f32)).astype(bf16)
        teach_ref[c] = out
        th[c, 0] = out[:, :SC]
        th[c, 1] = out[:, SC:]

        for h in range(2):
            far(c, h, True)
        for d in (1, 2, 3):
            xc(c, d).wait_send()
        zhc(c).wait_send()

    def py(c, d):
        ref = pg.at[c, g]
        s2 = lax.rem(c, 2)
        return rcopy(
            ref, ref, py_s.at[d - 1, s2], py_r.at[d - 1, c], z * 4 + (y + d) % 4, i
        )

    def pzc(c, d):
        ref = pg.at[c, z * 4 + (y + 4 - d) % 4]
        return rcopy(ref, ref, pz_s.at[d, lax.rem(c, 2)], pz_r.at[d, c], gz, i)

    def predict():
        load_proj.wait()
        pred[...] = jnp.tanh(
            jnp.dot(sin[...], proj[...], preferred_element_type=f32)
        ).reshape(2, C, 16, SC)

    def stage_v1(c):
        pltpu.make_async_copy(tgt.at[c], tgt.at[c], p_r.at[c]).wait()
        predicted = pred[:, c]
        mismatch = predicted - tgt[c].astype(f32)
        pg[c, g] = (mismatch * (1.0 - predicted * predicted)).astype(bf16)
        for d in (2, 1, 3):
            py(c, d).start()
        pzc(c, 0).start()
        for h in range(2):
            far(c, h, False)

    def stage_v2(c):
        for d in (1, 3, 2):
            py(c, d).wait_recv()
            pzc(c, d).start()

    def stage_v3(c):
        for d in range(4):
            pzc(c, d).wait_recv()
        rows = jnp.concatenate([sall[0, c], sall[1, c]], axis=0)
        pre = jnp.concatenate(
            [pg[c, :, 0].reshape(128, SC), pg[c, :, 1].reshape(128, SC)], axis=0
        )
        for n in range(4):
            cols = slice(n * 256, n * 256 + 256)
            gproj[cols, :] += lax.dot_general(
                rows[:, cols], pre, (((0,), (0,)), ((), ())), preferred_element_type=f32
            )
        for d in range(1, 4):
            py(c, d).wait_send()
        for d in range(4):
            pzc(c, d).wait_send()

    def a_copy(m, d):
        to = (i + d) % 16
        return rcopy(it.at[m, to // 2, to % 2], rr.at[m, 15 - d], a_s.at[d - 1], a_r.at[m], g, to)

    def b_copy(m, d):
        ref = rf.at[m, q, core]
        return rcopy(ref, ref, b_s.at[d - 1], b_r.at[m], g, (i + d) % 16)

    def each(copy, m, what):
        def body(d, _):
            what(copy(m, d))
            return 0
        lax.fori_loop(1, 16, body, 0)

    def stage_a1(m):
        own = pg[pl.ds(2 * m, 2), g].reshape(64, SC)
        for n in range(8):
            out = lax.dot_general(
                own, proj[n * 128:n * 128 + 128, :], (((1,), (1,)), ((), ())),
                preferred_element_type=f32,
            ).astype(bf16).reshape(2, 2, 16, 128)
            for b in range(2):
                it[m, n, b] = out[:, b]
        each(a_copy, m, lambda copy: copy.start())

    def stage_a2(m):
        pltpu.make_async_copy(rr.at[m], rr.at[m], a_r.at[m]).wait()
        out = it[m, q, core].astype(f32)
        for d in range(15):
            out = out + rr[m, d].astype(f32)
        rf[m, q, core] = out.astype(bf16)
        each(b_copy, m, lambda copy: copy.start())
        each(a_copy, m, lambda copy: copy.wait_send())

    def stage_a3(m):
        part = rr.at[m]
        pltpu.make_async_copy(part, part, b_r.at[m]).wait()
        for n in range(8):
            for b in range(2):
                gstu_ref[b, pl.ds(2 * m, 2), :, n * 128:n * 128 + 128] = rf[m, n, b]
        each(b_copy, m, lambda copy: copy.wait_send())

    gproj[...] = jnp.zeros_like(gproj)

    def tick(t, _):
        def run(stage, back):
            c = t - back

            @pl.when((c >= 0) & (c < C))
            def _():
                stage(c)

        def run_pair(stage, back):
            c = t - back

            @pl.when((c >= 0) & (c < C) & (c % 2 == 1))
            def _():
                stage(c // 2)

        run(wait_grp_sends, NS)
        for k in range(4):
            @pl.when(t == GROUPS[k][0])
            def _():
                t3(k).wait_recv()
        run(stage_g, 0)
        run(stage_r2, 1)
        run(stage_r4, 2)

        @pl.when(t == 3)
        def _():
            load_wd.wait()

        run(stage_dn, 3)
        run(stage_u2, 4)
        run(stage_v1, 5)
        run_pair(stage_a2, 6)

        @pl.when(t == 6)
        def _():
            t3(FAR).wait_recv()

        run(stage_v3, 6)
        run(stage_r1, 0)

        @pl.when(t == 0)
        def _():
            start_t3(1)
            scale_columns()

        run(stage_r3, 1)
        run(stage_r5, 2)
        run(stage_u1, 3)
        run(stage_u3, 4)
        run_pair(stage_a1, 5)
        run(stage_v2, 5)
        run_pair(stage_a3, 6)

        @pl.when(t == 1)
        def _():
            start_t3(2)
            pltpu.make_async_copy(
                sall.at[core, q, pl.ds(0, 112)], sall.at[core, q, pl.ds(0, 112)], s1_r
            ).wait()
            t1(FAR).start()

        @pl.when(t == 2)
        def _():
            start_t3(3)
            start_t2(FAR)
            predict()

        @pl.when(t == 4)
        def _():
            start_t3(FAR)
        return 0

    lax.fori_loop(0, C + 6, tick, 0)
    gproj_ref[...] = gproj[...].astype(bf16)

    for d in range(1, 8):
        ssq_copy(d).wait_send()
        s1_copy(d).wait_send()
    for k in range(5):
        t1(k).wait_send()
        for d in range(1, 4):
            t2(k, d).wait_send()
        t3(k).wait_send()

    @pl.when(teller)
    def _():
        for d in range(1, 16):
            inv_copy(d).wait_send()


def shards(tokens, norm_gain, gate_up_weight, down_weight, student_in, student_proj):
    vmem = pl.BlockSpec(memory_space=pltpu.VMEM)
    hbm = pl.BlockSpec(memory_space=pl.ANY)
    dma = pltpu.SemaphoreType.DMA
    teacher, grad_student, grad_proj = pl.pallas_call(
        kernel,
        out_shape=(
            jax.ShapeDtypeStruct((C, 16, KB), bf16),
            jax.ShapeDtypeStruct((2, C, 16, SD), bf16),
            jax.ShapeDtypeStruct((SD, SC), bf16),
        ),
        in_specs=[vmem, vmem, hbm, hbm, hbm, hbm],
        out_specs=(vmem, vmem, vmem),
        scratch_shapes=[
            pltpu.VMEM((2, KB, FB), bf16),
            pltpu.VMEM((FB, KB), bf16),
            pltpu.VMEM((SD, SC), bf16),
            pltpu.VMEM((256, SD), bf16),
            pltpu.VMEM((2, C, 16, SC), f32),
            pltpu.VMEM((C, 2, 8, 16, KB), bf16),
            pltpu.VMEM((2, 8, 128, SD), bf16),
            pltpu.VMEM((8, 128), f32),
            pltpu.VMEM((7, 8, 128), f32),
            pltpu.VMEM((8, 128), f32),
            pltpu.VMEM((2, 8, 128), f32),
            pltpu.VMEM((2, C, 16, 128), f32),
            pltpu.VMEM((NS, 4, 2, HR, F2), bf16),
            pltpu.VMEM((NS, 2, HR, F2), bf16),
            pltpu.VMEM((NS, 2, 2, HR, F2), bf16),
            pltpu.VMEM((NS, HR, F2), bf16),
            pltpu.VMEM((NS, 4, 2, HR, FB), bf16),
            pltpu.VMEM((2, 2, 128, KB), bf16),
            pltpu.VMEM((C, 128, KB), bf16),
            pltpu.VMEM((2, 4, 2, 16, KB), bf16),
            pltpu.VMEM((C, 3, 2, 16, KB), bf16),
            pltpu.VMEM((2, 16, KB), bf16),
            pltpu.VMEM((C, 16, KB), bf16),
            pltpu.VMEM((C, 2, 16, SC), bf16),
            pltpu.VMEM((C, 2, 16, SC), bf16),
            pltpu.VMEM((C, 8, 2, 16, SC), bf16),
            pltpu.VMEM((SD, SC), f32),
            pltpu.VMEM((4, 8, 2, 2, 16, 128), bf16),
            pltpu.VMEM((4, 15, 2, 16, 128), bf16),
            pltpu.VMEM((4, 8, 2, 2, 16, 128), bf16),
            dma((4,)),
            dma((7,)), dma(()),
            dma((15,)), dma((2,)),
            dma((7,)), dma(()),
            dma((5,)), dma((5,)),
            dma((5, 3)), dma((5, 3)),
            dma((5,)), dma((5,)),
            dma((7, NS)), dma((7, NS)),
            dma((8, NS)), dma((8, NS)),
            dma((2,)), dma((C,)),
            dma((3, 2)), dma((3, C)),
            dma((2,)), dma((C,)),
            dma((2,)), dma((C,)),
            dma((3, 2)), dma((3, C)),
            dma((4, 2)), dma((4, C)),
            dma((15,)), dma((4,)),
            dma((15,)), dma((4,)),
        ],
        compiler_params=pltpu.CompilerParams(
            collective_id=0, has_side_effects=True, vmem_limit_bytes=62 * 1024 * 1024
        ),
    )(tokens, norm_gain.reshape(1, KB), gate_up_weight, down_weight, student_in, student_proj)
    return (
        teacher.reshape(128, KB), grad_student.reshape(256, SD).astype(f32), grad_proj.astype(f32)
    )


def solution(mesh):
    return jax.shard_map(
        shards,
        mesh=mesh,
        in_specs=(
            P("inner", "grp"),
            P("grp"),
            P(None, "grp", "inner"),
            P("inner", "grp"),
            P("grp", None),
            P(None, "inner"),
        ),
        out_specs=(P("inner", "grp"), P("grp", None), P(None, "inner")),
        check_vma=False,
    )
```

```python
import jax
import jax.numpy as jnp
from jax import lax
from jax.experimental import pallas as pl
from jax.experimental.pallas import tpu as pltpu
from jax.sharding import PartitionSpec as P

D = 8192
KB = 1024
FB = 1792
F2 = 2 * FB
SD = 1024
SC = 512
C = 8
MC = 256
HR = 32
NS = 4
GROUPS = ((0, 1), (1, 1), (2, 2), (4, 4))
FAR = 4
f32, bf16 = jnp.float32, jnp.bfloat16
MESH = pl.DeviceIdType.MESH


def kernel(
    tok_ref, gain_ref, w_hbm, wd_hbm, sin_hbm, proj_hbm,
    teach_ref, gstu_ref, gproj_ref,
    w, wd, proj, sin, pred, xb, sall, ssq, ssqr, inv_own, inv_line, inv,
    gs, ra, rb, rz, hb, ps, rc, px, rx, pz, rzh, th, tgt, pg, gproj, it, rr, rf,
    lsem, ssq_s, ssq_r, inv_s, inv_r, s1_s, s1_r, t0_s, t0_r, t1_s, t1_r, t2_s, t2_r, t3_s, t3_r,
    rs_s, rs_r, hz_s, hz_r, c_s, c_r, x_s, x_r, zh_s, zh_r, p_s, p_r,
    py_s, py_r, pz_s, pz_r, a_s, a_r, b_s, b_r,
):
    g = lax.axis_index("grp")
    i = lax.axis_index("inner")
    z, y = g // 4, g % 4
    x, core, q = i // 4, i % 2, i // 2
    yp, ym, yd = (y + 1) % 4, (y + 3) % 4, (y + 2) % 4
    gp, gm = z * 4 + yp, z * 4 + ym
    gz = (1 - z) * 4 + y
    oz = 1 - z
    zh = q % 2
    izh = x * 4 + (1 - zh) * 2 + core
    icore = x * 4 + zh * 2 + (1 - core)
    pos = core * 8 + q
    me_far = g == q

    def rcopy(src, dst, ss, rs, dg, di):
        return pltpu.make_async_remote_copy(
            src_ref=src, dst_ref=dst, send_sem=ss, recv_sem=rs,
            device_id=(dg, di), device_id_type=MESH,
        )

    load_w = pltpu.make_async_copy(w_hbm, w, lsem.at[0])
    load_wd = pltpu.make_async_copy(wd_hbm, wd, lsem.at[1])
    load_proj = pltpu.make_async_copy(proj_hbm, proj, lsem.at[2])
    rows16 = pl.ds(pl.multiple_of(pos * 16, 16), 16)
    my16 = pl.ds(pl.multiple_of(g * 16, 16), 16)
    load_sin = pltpu.make_async_copy(sin_hbm, sin, lsem.at[3])
    load_w.start()
    load_wd.start()
    load_proj.start()
    load_sin.start()

    barrier = pltpu.get_barrier_semaphore()

    def greet_grp(d, _):
        pl.semaphore_signal(barrier, inc=1, device_id=((g + d) % 8, i), device_id_type=MESH)
        return 0

    def greet_inner(d, _):
        pl.semaphore_signal(barrier, inc=1, device_id=(g, (i + d) % 16), device_id_type=MESH)
        return 0

    lax.fori_loop(1, 8, greet_grp, 0)
    lax.fori_loop(1, 16, greet_inner, 0)
    for h in range(2):
        @pl.when(jnp.logical_not(me_far & (core == h)))
        def _():
            pl.semaphore_signal(barrier, inc=1, device_id=(q, 2 * g + h), device_id_type=MESH)

    values = tok_ref[...].astype(f32)
    total = jnp.sum(values * values, axis=1, keepdims=True)
    ssq[...] = jnp.broadcast_to(total, (128, 128)).T[0:8]

    xb[:, core, q] = (values * gain_ref[...].astype(f32).reshape(1, KB)).astype(bf16).reshape(8, 16, KB)
    pl.semaphore_wait(barrier, jnp.where(me_far, 23, 24))

    def ssq_copy(d):
        return rcopy(ssq, ssqr.at[7 - d], ssq_s.at[d - 1], ssq_r, (g + d) % 8, i)

    def s1_copy(d):
        return rcopy(
            sin.at[rows16], sall.at[core, q, my16], s1_s.at[d - 1], s1_r, (g + d) % 8, i
        )

    teller = g == ((q // 2) % 2) * 4 + core * 2 + q // 4

    def inv_copy(d):
        return rcopy(inv_own, inv_line.at[q % 2], inv_s.at[d - 1], inv_r.at[q % 2], g, (i + d) % 16)

    def scales():
        pltpu.make_async_copy(ssqr, ssqr, ssq_r).wait()
        line = ssq[...]
        for d in range(7):
            line = line + ssqr[d]
        inv_own[...] = lax.rsqrt(line / D + 1e-05)

        @pl.when(teller)
        def _():
            for d in range(1, 16):
                inv_copy(d).start()

    def scale_columns():
        for k in range(2):
            mine = teller & (q % 2 == k)

            @pl.when(mine)
            def _():
                inv_line[k] = inv_own[...]

            @pl.when(jnp.logical_not(mine))
            def _():
                pltpu.make_async_copy(inv_line.at[k], inv_line.at[k], inv_r.at[k]).wait()

            inv[k] = jnp.broadcast_to(inv_line[k, 0:1], (128, 128)).T.reshape(C, 16, 128)

    x2 = pl.ds(pl.multiple_of(x * 2, 2), 2)

    def t0(d):
        ref = xb.at[0, core, q]
        return rcopy(ref, ref, t0_s.at[d - 1], t0_r.at[d - 1], g, (i + 2 * d) % 16)

    def t1(k):
        if k == FAR:
            ref = sall.at[core, q]
        else:
            ref = xb.at[pl.ds(GROUPS[k][0], GROUPS[k][1]), core, q]
        return rcopy(ref, ref, t1_s.at[k], t1_r.at[k], g, izh)

    def t2(k, d):
        if k == FAR:
            ref = sall.at[core, x2]
        else:
            ref = xb.at[pl.ds(GROUPS[k][0], GROUPS[k][1]), core, x2]
        return rcopy(ref, ref, t2_s.at[k, d - 1], t2_r.at[k, d - 1], g, (i + 4 * d) % 16)

    def t3(k):
        if k == FAR:
            ref = sall.at[core]
        else:
            ref = xb.at[pl.ds(GROUPS[k][0], GROUPS[k][1]), core]
        return rcopy(ref, ref, t3_s.at[k], t3_r.at[k], g, icore)

    def start_t2(k):
        t1(k).wait_recv()
        for d in (2, 1, 3):
            t2(k, d).start()

    def start_t3(k):
        for d in (1, 3, 2):
            t2(k, d).wait_recv()
        t3(k).start()

    for d in (4, 3, 5, 2, 6, 1, 7):
        t0(d).start()
    for k in range(1, 4):
        t1(k).start()
    for d in range(1, 8):
        ssq_copy(d).start()
    for d in range(1, 8):
        t0(d).wait_recv()
    t3(0).start()
    scales()
    for k in range(1, 4):
        start_t2(k)
    load_sin.wait()
    sall[core, q, my16] = sin[rows16]
    for d in range(1, 8):
        s1_copy(d).start()
    load_w.wait()

    def slot(c):
        return lax.rem(c, NS)

    def a_p(c):
        s = slot(c)
        return rcopy(gs.at[s, yd, 0], ra.at[s, 0], rs_s.at[0, s], rs_r.at[0, s], gp, i)

    def a_m(c):
        s = slot(c)
        return rcopy(gs.at[s, yd, 1], ra.at[s, 1], rs_s.at[1, s], rs_r.at[1, s], gm, i)

    def b1_p(c):
        s = slot(c)
        return rcopy(gs.at[s, yp, 1], rb.at[s, 0, 1], rs_s.at[2, s], rs_r.at[2, s], gp, i)

    def b1_m(c):
        s = slot(c)
        return rcopy(gs.at[s, ym, 0], rb.at[s, 1, 0], rs_s.at[3, s], rs_r.at[3, s], gm, i)

    def b2_p(c):
        s = slot(c)
        return rcopy(gs.at[s, yp, 0], rb.at[s, 0, 0], rs_s.at[4, s], rs_r.at[4, s], gp, i)

    def b2_m(c):
        s = slot(c)
        return rcopy(gs.at[s, ym, 1], rb.at[s, 1, 1], rs_s.at[5, s], rs_r.at[5, s], gm, i)

    def zc(c):
        s = slot(c)
        return rcopy(gs.at[s, y, oz], rz.at[s], rs_s.at[6, s], rs_r.at[6, s], gz, i)

    def e_p(c):
        s = slot(c)
        ref = hb.at[s, y, z]
        return rcopy(ref, ref, hz_s.at[0, s], hz_r.at[0, s], gp, i)

    def e_m(c):
        s = slot(c)
        ref = hb.at[s, y, z]
        return rcopy(ref, ref, hz_s.at[1, s], hz_r.at[1, s], gm, i)

    def f_p(c):
        s = slot(c)
        ref = hb.at[s, ym, z, pl.ds(0, 16)]
        return rcopy(ref, ref, hz_s.at[2, s], hz_r.at[2, s], gp, i)

    def f_m(c):
        s = slot(c)
        ref = hb.at[s, yp, z, pl.ds(16, 16)]
        return rcopy(ref, ref, hz_s.at[3, s], hz_r.at[3, s], gm, i)

    def ez(c, block, n):
        s = slot(c)
        ref = hb.at[s, block, z]
        return rcopy(ref, ref, hz_s.at[4 + n, s], hz_r.at[4 + n, s], gz, i)

    def wait_grp_sends(c):
        for copy in (a_p, a_m, b1_p, b1_m, b2_p, b2_m, zc, e_p, e_m, f_p, f_m):
            copy(c).wait_send()
        for n, block in enumerate((y, ym, yp, yd)):
            ez(c, block, n).wait_send()

    def stage_g(c):
        s = slot(c)
        rows = xb.at[c].reshape(MC, KB)
        for k in range(2):
            @pl.loop(0, 7)
            def _(n):
                cols = pl.ds(pl.multiple_of(n * 256, 256), 256)
                out = jnp.dot(rows[...], w[k, :, cols], preferred_element_type=f32)
                gs[s, :, :, :, pl.ds(pl.multiple_of(k * FB + n * 256, 256), 256)] = (
                    out.astype(bf16).reshape(4, 2, HR, 256)
                )
        a_p(c).start()
        a_m(c).start()
        b1_p(c).start()
        b1_m(c).start()

    def stage_r1(c):
        s = slot(c)
        a_p(c).wait_recv()
        gs[s, yp, 0] = (gs[s, yp, 0].astype(f32) + ra[s, 0].astype(f32)).astype(bf16)
        b2_p(c).start()
        a_m(c).wait_recv()
        gs[s, ym, 1] = (gs[s, ym, 1].astype(f32) + ra[s, 1].astype(f32)).astype(bf16)
        b2_m(c).start()

    def stage_r2(c):
        s = slot(c)
        for copy in (b1_p, b1_m, b2_p, b2_m):
            copy(c).wait_recv()
        gs[s, y, oz] = (
            gs[s, y, oz].astype(f32) + rb[s, 0, oz].astype(f32) + rb[s, 1, oz].astype(f32)
        ).astype(bf16)
        zc(c).start()

    def stage_r3(c):
        s = slot(c)
        zc(c).wait_recv()

        def part(cols):
            return (
                gs[s, y, z, :, cols].astype(f32) + rb[s, 0, z, :, cols].astype(f32)
                + rb[s, 1, z, :, cols].astype(f32) + rz[s, :, cols].astype(f32)
            )

        scale = jnp.concatenate([inv[0, c][:, 0:1], inv[1, c][:, 0:1]], axis=0)
        for n in range(7):
            gate = part(pl.ds(n * 256, 256)) * scale
            up = part(pl.ds(FB + n * 256, 256)) * scale
            hb[s, y, z, :, pl.ds(n * 256, 256)] = (gate / (1.0 + jnp.exp(-gate)) * up).astype(bf16)
        e_p(c).start()
        e_m(c).start()
        ez(c, y, 0).start()

    def stage_r4(c):
        e_p(c).wait_recv()
        f_p(c).start()
        e_m(c).wait_recv()
        f_m(c).start()
        ez(c, ym, 1).start()
        ez(c, yp, 2).start()

    def stage_r5(c):
        f_p(c).wait_recv()
        f_m(c).wait_recv()
        ez(c, yd, 3).start()

    def cc(c):
        s = lax.rem(c, 2)
        return rcopy(ps.at[s, 1 - core], rc.at[c], c_s.at[s], c_r.at[c], g, icore)

    def xc(c, d):
        s = lax.rem(c, 2)
        return rcopy(
            px.at[s, (x + d) % 4], rx.at[c, d - 1], x_s.at[d - 1, s], x_r.at[d - 1, c],
            g, (i + 4 * d) % 16,
        )

    def zhc(c):
        s = lax.rem(c, 2)
        return rcopy(pz.at[s], rzh.at[c], zh_s.at[s], zh_r.at[c], g, izh)

    def stage_dn(c):
        s, s2 = slot(c), lax.rem(c, 2)
        for n, block in enumerate((y, ym, yp, yd)):
            ez(c, block, n).wait_recv()
        rows = hb.at[s].reshape(MC, FB)

        @pl.loop(0, 4)
        def _(n):
            cols = pl.ds(pl.multiple_of(n * 256, 256), 256)
            out = jnp.dot(rows[...], wd[:, cols], preferred_element_type=f32)
            ps[s2, :, :, cols] = out.astype(bf16).reshape(2, 128, 256)

        cc(c).start()

    def stage_u1(c):
        s2 = lax.rem(c, 2)
        cc(c).wait_recv()
        px[s2] = (ps[s2, core].astype(f32) + rc[c].astype(f32)).astype(bf16).reshape(4, 2, 16, KB)
        for d in (2, 1, 3):
            xc(c, d).start()
        cc(c).wait_send()

    def sum_x(c, half):
        s2 = lax.rem(c, 2)
        out = px[s2, x, half].astype(f32)
        for d in range(3):
            out = out + rx[c, d, half].astype(f32)
        return out

    def stage_u2(c):
        for d in (1, 3, 2):
            xc(c, d).wait_recv()
        pz[lax.rem(c, 2)] = sum_x(c, 1 - zh).astype(bf16)
        zhc(c).start()

    def far_copy(c, h):
        return rcopy(th.at[c, h], tgt.at[c, core], p_s.at[h], p_r.at[c], q, 2 * g + h)

    def far(c, h, begin):
        own = me_far & (core == h)

        @pl.when(jnp.logical_not(own))
        def _():
            if begin:
                far_copy(c, h).start()
            else:
                far_copy(c, h).wait_send()

        if begin:
            @pl.when(own)
            def _():
                pltpu.make_async_copy(th.at[c, h], tgt.at[c, core], p_r.at[c]).start()

    def stage_u3(c):
        zhc(c).wait_recv()
        out = (sum_x(c, zh) + rzh[c].astype(f32)).astype(bf16)
        teach_ref[c] = out
        th[c, 0] = out[:, :SC]
        th[c, 1] = out[:, SC:]

        for h in range(2):
            far(c, h, True)
        for d in (1, 2, 3):
            xc(c, d).wait_send()
        zhc(c).wait_send()

    def py(c, d):
        ref = pg.at[c, g]
        s2 = lax.rem(c, 2)
        return rcopy(
            ref, ref, py_s.at[d - 1, s2], py_r.at[d - 1, c], z * 4 + (y + d) % 4, i
        )

    def pzc(c, d):
        ref = pg.at[c, z * 4 + (y + 4 - d) % 4]
        return rcopy(ref, ref, pz_s.at[d, lax.rem(c, 2)], pz_r.at[d, c], gz, i)

    def predict():
        load_proj.wait()
        pred[...] = jnp.tanh(
            jnp.dot(sin[...], proj[...], preferred_element_type=f32)
        ).reshape(2, C, 16, SC)

    def stage_v1(c):
        pltpu.make_async_copy(tgt.at[c], tgt.at[c], p_r.at[c]).wait()
        predicted = pred[:, c]
        mismatch = predicted - tgt[c].astype(f32)
        pg[c, g] = (mismatch * (1.0 - predicted * predicted)).astype(bf16)
        for d in (2, 1, 3):
            py(c, d).start()
        pzc(c, 0).start()
        for h in range(2):
            far(c, h, False)

    def stage_v2(c):
        for d in (1, 3, 2):
            py(c, d).wait_recv()
            pzc(c, d).start()

    def stage_v3(c):
        for d in range(4):
            pzc(c, d).wait_recv()
        rows = jnp.concatenate([sall[0, c], sall[1, c]], axis=0)
        pre = jnp.concatenate(
            [pg[c, :, 0].reshape(128, SC), pg[c, :, 1].reshape(128, SC)], axis=0
        )
        for n in range(4):
            cols = slice(n * 256, n * 256 + 256)
            gproj[cols, :] += lax.dot_general(
                rows[:, cols], pre, (((0,), (0,)), ((), ())), preferred_element_type=f32
            )
        for d in range(1, 4):
            py(c, d).wait_send()
        for d in range(4):
            pzc(c, d).wait_send()

    def a_copy(m, d):
        to = (i + d) % 16
        return rcopy(it.at[m, to // 2, to % 2], rr.at[m, 15 - d], a_s.at[d - 1], a_r.at[m], g, to)

    def b_copy(m, d):
        ref = rf.at[m, q, core]
        return rcopy(ref, ref, b_s.at[d - 1], b_r.at[m], g, (i + d) % 16)

    def each(copy, m, what):
        def body(d, _):
            what(copy(m, d))
            return 0
        lax.fori_loop(1, 16, body, 0)

    def stage_a1(m):
        own = pg[pl.ds(2 * m, 2), g].reshape(64, SC)
        for n in range(8):
            out = lax.dot_general(
                own, proj[n * 128:n * 128 + 128, :], (((1,), (1,)), ((), ())),
                preferred_element_type=f32,
            ).astype(bf16).reshape(2, 2, 16, 128)
            for b in range(2):
                it[m, n, b] = out[:, b]
        each(a_copy, m, lambda copy: copy.start())

    def stage_a2(m):
        pltpu.make_async_copy(rr.at[m], rr.at[m], a_r.at[m]).wait()
        out = it[m, q, core].astype(f32)
        for d in range(15):
            out = out + rr[m, d].astype(f32)
        rf[m, q, core] = out.astype(bf16)
        each(b_copy, m, lambda copy: copy.start())
        each(a_copy, m, lambda copy: copy.wait_send())

    def stage_a3(m):
        part = rr.at[m]
        pltpu.make_async_copy(part, part, b_r.at[m]).wait()
        for n in range(8):
            for b in range(2):
                gstu_ref[b, pl.ds(2 * m, 2), :, n * 128:n * 128 + 128] = rf[m, n, b]
        each(b_copy, m, lambda copy: copy.wait_send())

    gproj[...] = jnp.zeros_like(gproj)

    def tick(t, _):
        def run(stage, back):
            c = t - back

            @pl.when((c >= 0) & (c < C))
            def _():
                stage(c)

        def run_pair(stage, back):
            c = t - back

            @pl.when((c >= 0) & (c < C) & (c % 2 == 1))
            def _():
                stage(c // 2)

        run(wait_grp_sends, NS)
        for k in range(4):
            @pl.when(t == GROUPS[k][0])
            def _():
                t3(k).wait_recv()
        run(stage_g, 0)
        run(stage_r2, 1)
        run(stage_r4, 2)

        @pl.when(t == 3)
        def _():
            load_wd.wait()

        run(stage_dn, 3)
        run(stage_u2, 4)
        run(stage_v1, 5)
        run_pair(stage_a2, 6)

        @pl.when(t == 6)
        def _():
            t3(FAR).wait_recv()

        run(stage_v3, 6)
        run(stage_r1, 0)

        @pl.when(t == 0)
        def _():
            start_t3(1)
            scale_columns()

        run(stage_r3, 1)
        run(stage_r5, 2)
        run(stage_u1, 3)
        run(stage_u3, 4)
        run_pair(stage_a1, 5)
        run(stage_v2, 5)
        run_pair(stage_a3, 6)

        @pl.when(t == 1)
        def _():
            start_t3(2)
            pltpu.make_async_copy(
                sall.at[core, q, pl.ds(0, 112)], sall.at[core, q, pl.ds(0, 112)], s1_r
            ).wait()
            t1(FAR).start()

        @pl.when(t == 2)
        def _():
            start_t3(3)
            start_t2(FAR)
            predict()

        @pl.when(t == 4)
        def _():
            start_t3(FAR)
        return 0

    lax.fori_loop(0, C + 6, tick, 0)
    gproj_ref[...] = gproj[...].astype(bf16)

    for d in range(1, 8):
        ssq_copy(d).wait_send()
        s1_copy(d).wait_send()
    for d in range(1, 8):
        t0(d).wait_send()
    for k in range(1, 5):
        t1(k).wait_send()
        for d in range(1, 4):
            t2(k, d).wait_send()
    for k in range(5):
        t3(k).wait_send()

    @pl.when(teller)
    def _():
        for d in range(1, 16):
            inv_copy(d).wait_send()


def widen(a_ref, b_ref, c_ref, a_out, b_out, c_out):
    a_out[...] = a_ref[...]
    b_out[...] = b_ref[...].astype(f32)
    c_out[...] = c_ref[...].astype(f32)


def shards(tokens, norm_gain, gate_up_weight, down_weight, student_in, student_proj):
    vmem = pl.BlockSpec(memory_space=pltpu.VMEM)
    hbm = pl.BlockSpec(memory_space=pl.ANY)
    dma = pltpu.SemaphoreType.DMA
    teacher, grad_student, grad_proj = pl.pallas_call(
        kernel,
        out_shape=(
            jax.ShapeDtypeStruct((C, 16, KB), bf16),
            jax.ShapeDtypeStruct((2, C, 16, SD), bf16),
            jax.ShapeDtypeStruct((SD, SC), bf16),
        ),
        in_specs=[vmem, vmem, hbm, hbm, hbm, hbm],
        out_specs=(vmem, vmem, vmem),
        scratch_shapes=[
            pltpu.VMEM((2, KB, FB), bf16),
            pltpu.VMEM((FB, KB), bf16),
            pltpu.VMEM((SD, SC), bf16),
            pltpu.VMEM((256, SD), bf16),
            pltpu.VMEM((2, C, 16, SC), f32),
            pltpu.VMEM((C, 2, 8, 16, KB), bf16),
            pltpu.VMEM((2, 8, 128, SD), bf16),
            pltpu.VMEM((8, 128), f32),
            pltpu.VMEM((7, 8, 128), f32),
            pltpu.VMEM((8, 128), f32),
            pltpu.VMEM((2, 8, 128), f32),
            pltpu.VMEM((2, C, 16, 128), f32),
            pltpu.VMEM((NS, 4, 2, HR, F2), bf16),
            pltpu.VMEM((NS, 2, HR, F2), bf16),
            pltpu.VMEM((NS, 2, 2, HR, F2), bf16),
            pltpu.VMEM((NS, HR, F2), bf16),
            pltpu.VMEM((NS, 4, 2, HR, FB), bf16),
            pltpu.VMEM((2, 2, 128, KB), bf16),
            pltpu.VMEM((C, 128, KB), bf16),
            pltpu.VMEM((2, 4, 2, 16, KB), bf16),
            pltpu.VMEM((C, 3, 2, 16, KB), bf16),
            pltpu.VMEM((2, 16, KB), bf16),
            pltpu.VMEM((C, 16, KB), bf16),
            pltpu.VMEM((C, 2, 16, SC), bf16),
            pltpu.VMEM((C, 2, 16, SC), bf16),
            pltpu.VMEM((C, 8, 2, 16, SC), bf16),
            pltpu.VMEM((SD, SC), f32),
            pltpu.VMEM((4, 8, 2, 2, 16, 128), bf16),
            pltpu.VMEM((4, 15, 2, 16, 128), bf16),
            pltpu.VMEM((4, 8, 2, 2, 16, 128), bf16),
            dma((4,)),
            dma((7,)), dma(()),
            dma((15,)), dma((2,)),
            dma((7,)), dma(()),
            dma((7,)), dma((7,)),
            dma((5,)), dma((5,)),
            dma((5, 3)), dma((5, 3)),
            dma((5,)), dma((5,)),
            dma((7, NS)), dma((7, NS)),
            dma((8, NS)), dma((8, NS)),
            dma((2,)), dma((C,)),
            dma((3, 2)), dma((3, C)),
            dma((2,)), dma((C,)),
            dma((2,)), dma((C,)),
            dma((3, 2)), dma((3, C)),
            dma((4, 2)), dma((4, C)),
            dma((15,)), dma((4,)),
            dma((15,)), dma((4,)),
        ],
        compiler_params=pltpu.CompilerParams(
            collective_id=0, has_side_effects=True, vmem_limit_bytes=62 * 1024 * 1024
        ),
    )(tokens, norm_gain, gate_up_weight, down_weight, student_in, student_proj)
    return pl.pallas_call(
        widen,
        grid=(4,),
        out_shape=(
            jax.ShapeDtypeStruct((128, KB), bf16),
            jax.ShapeDtypeStruct((256, SD), f32),
            jax.ShapeDtypeStruct((SD, SC), f32),
        ),
        in_specs=[
            pl.BlockSpec((32, KB), lambda n: (n, 0)),
            pl.BlockSpec((64, SD), lambda n: (n, 0)),
            pl.BlockSpec((256, SC), lambda n: (n, 0)),
        ],
        out_specs=(
            pl.BlockSpec((32, KB), lambda n: (n, 0)),
            pl.BlockSpec((64, SD), lambda n: (n, 0)),
            pl.BlockSpec((256, SC), lambda n: (n, 0)),
        ),
    )(teacher.reshape(128, KB), grad_student.reshape(256, SD), grad_proj)


def solution(mesh):
    return jax.shard_map(
        shards,
        mesh=mesh,
        in_specs=(
            P("inner", "grp"),
            P("grp"),
            P(None, "grp", "inner"),
            P("inner", "grp"),
            P("grp", None),
            P(None, "inner"),
        ),
        out_specs=(P("inner", "grp"), P("grp", None), P(None, "inner")),
        check_vma=False,
    )
```

```python
import jax
import jax.numpy as jnp
from jax import lax
from jax.experimental import pallas as pl
from jax.experimental.pallas import tpu as pltpu
from jax.sharding import PartitionSpec as P

D = 8192
KB = 1024
FB = 1792
F2 = 2 * FB
SD = 1024
SC = 512
C = 8
MC = 256
HR = 32
NS = 4
GROUPS = ((0, 1), (1, 1), (2, 2), (4, 4))
FAR = 4
f32, bf16 = jnp.float32, jnp.bfloat16
MESH = pl.DeviceIdType.MESH


def kernel(
    tok_ref, gain_ref, w_hbm, wd_hbm, sin_hbm, proj_hbm,
    teach_ref, gstu_ref, gproj_ref,
    w, wd, proj, sin, pred, xb, sall, ssq, ssqr, inv_own, inv_line, inv,
    gs, ra, rb, rz, hb, ps, rc, px, rx, pz, rzh, th, tgt, pg, gproj, it, rr, rf,
    lsem, ssq_s, ssq_r, inv_s, inv_r, s1_s, s1_r, t0_s, t0_r, t1_s, t1_r, t2_s, t2_r, t3_s, t3_r,
    rs_s, rs_r, hz_s, hz_r, c_s, c_r, x_s, x_r, zh_s, zh_r, p_s, p_r,
    py_s, py_r, pz_s, pz_r, a_s, a_r, b_s, b_r,
):
    g = lax.axis_index("grp")
    i = lax.axis_index("inner")
    z, y = g // 4, g % 4
    x, core, q = i // 4, i % 2, i // 2
    yp, ym, yd = (y + 1) % 4, (y + 3) % 4, (y + 2) % 4
    gp, gm = z * 4 + yp, z * 4 + ym
    gz = (1 - z) * 4 + y
    oz = 1 - z
    zh = q % 2
    izh = x * 4 + (1 - zh) * 2 + core
    icore = x * 4 + zh * 2 + (1 - core)
    pos = core * 8 + q
    me_far = g == q

    def rcopy(src, dst, ss, rs, dg, di):
        return pltpu.make_async_remote_copy(
            src_ref=src, dst_ref=dst, send_sem=ss, recv_sem=rs,
            device_id=(dg, di), device_id_type=MESH,
        )

    load_w = pltpu.make_async_copy(w_hbm, w, lsem.at[0])
    load_wd = pltpu.make_async_copy(wd_hbm, wd, lsem.at[1])
    load_proj = pltpu.make_async_copy(proj_hbm, proj, lsem.at[2])
    rows16 = pl.ds(pl.multiple_of(pos * 16, 16), 16)
    my16 = pl.ds(pl.multiple_of(g * 16, 16), 16)
    load_sin = pltpu.make_async_copy(sin_hbm, sin, lsem.at[3])
    load_w.start()
    load_wd.start()
    load_proj.start()
    load_sin.start()

    barrier = pltpu.get_barrier_semaphore()

    def greet_grp(d, _):
        pl.semaphore_signal(barrier, inc=1, device_id=((g + d) % 8, i), device_id_type=MESH)
        return 0

    def greet_inner(d, _):
        pl.semaphore_signal(barrier, inc=1, device_id=(g, (i + d) % 16), device_id_type=MESH)
        return 0

    lax.fori_loop(1, 8, greet_grp, 0)
    lax.fori_loop(1, 16, greet_inner, 0)
    for h in range(2):
        @pl.when(jnp.logical_not(me_far & (core == h)))
        def _():
            pl.semaphore_signal(barrier, inc=1, device_id=(q, 2 * g + h), device_id_type=MESH)

    values = tok_ref[...].astype(f32)
    total = jnp.sum(values * values, axis=1, keepdims=True)
    ssq[...] = jnp.broadcast_to(total, (128, 128)).T[0:8]

    xb[:, core, q] = (values * gain_ref[...].astype(f32).reshape(1, KB)).astype(bf16).reshape(8, 16, KB)
    pl.semaphore_wait(barrier, jnp.where(me_far, 23, 24))

    def ssq_copy(d):
        return rcopy(ssq, ssqr.at[7 - d], ssq_s.at[d - 1], ssq_r, (g + d) % 8, i)

    def s1_copy(d):
        return rcopy(
            sin.at[rows16], sall.at[core, q, my16], s1_s.at[d - 1], s1_r, (g + d) % 8, i
        )

    teller = g == ((q // 2) % 2) * 4 + core * 2 + q // 4

    def inv_copy(d):
        return rcopy(inv_own, inv_line.at[q % 2], inv_s.at[d - 1], inv_r.at[q % 2], g, (i + d) % 16)

    def scales():
        pltpu.make_async_copy(ssqr, ssqr, ssq_r).wait()
        line = ssq[...]
        for d in range(7):
            line = line + ssqr[d]
        inv_own[...] = lax.rsqrt(line / D + 1e-05)

        @pl.when(teller)
        def _():
            for d in range(1, 16):
                inv_copy(d).start()

    def scale_columns():
        for k in range(2):
            mine = teller & (q % 2 == k)

            @pl.when(mine)
            def _():
                inv_line[k] = inv_own[...]

            @pl.when(jnp.logical_not(mine))
            def _():
                pltpu.make_async_copy(inv_line.at[k], inv_line.at[k], inv_r.at[k]).wait()

            inv[k] = jnp.broadcast_to(inv_line[k, 0:1], (128, 128)).T.reshape(C, 16, 128)

    x2 = pl.ds(pl.multiple_of(x * 2, 2), 2)

    def t0(d):
        ref = xb.at[0, core, q]
        return rcopy(ref, ref, t0_s.at[d - 1], t0_r.at[d - 1], g, (i + 2 * d) % 16)

    def t1(k):
        if k == FAR:
            ref = sall.at[core, q]
        else:
            ref = xb.at[pl.ds(GROUPS[k][0], GROUPS[k][1]), core, q]
        return rcopy(ref, ref, t1_s.at[k], t1_r.at[k], g, izh)

    def t2(k, d):
        if k == FAR:
            ref = sall.at[core, x2]
        else:
            ref = xb.at[pl.ds(GROUPS[k][0], GROUPS[k][1]), core, x2]
        return rcopy(ref, ref, t2_s.at[k, d - 1], t2_r.at[k, d - 1], g, (i + 4 * d) % 16)

    def t3(k):
        if k == FAR:
            ref = sall.at[core]
        else:
            ref = xb.at[pl.ds(GROUPS[k][0], GROUPS[k][1]), core]
        return rcopy(ref, ref, t3_s.at[k], t3_r.at[k], g, icore)

    def start_t2(k):
        t1(k).wait_recv()
        for d in (2, 1, 3):
            t2(k, d).start()

    def start_t3(k):
        for d in (1, 3, 2):
            t2(k, d).wait_recv()
        t3(k).start()

    for d in (4, 3, 5, 2, 6, 1, 7):
        t0(d).start()
    for k in range(1, 4):
        t1(k).start()
    for d in range(1, 8):
        ssq_copy(d).start()
    for d in range(1, 8):
        t0(d).wait_recv()
    t3(0).start()
    scales()
    for k in range(1, 4):
        start_t2(k)
    load_sin.wait()
    sall[core, q, my16] = sin[rows16]
    for d in range(1, 8):
        s1_copy(d).start()
    load_w.wait()

    def slot(c):
        return lax.rem(c, NS)

    def a_p(c):
        s = slot(c)
        return rcopy(gs.at[s, yd, 0], ra.at[s, 0], rs_s.at[0, s], rs_r.at[0, s], gp, i)

    def a_m(c):
        s = slot(c)
        return rcopy(gs.at[s, yd, 1], ra.at[s, 1], rs_s.at[1, s], rs_r.at[1, s], gm, i)

    def b1_p(c):
        s = slot(c)
        return rcopy(gs.at[s, yp, 1], rb.at[s, 0, 1], rs_s.at[2, s], rs_r.at[2, s], gp, i)

    def b1_m(c):
        s = slot(c)
        return rcopy(gs.at[s, ym, 0], rb.at[s, 1, 0], rs_s.at[3, s], rs_r.at[3, s], gm, i)

    def b2_p(c):
        s = slot(c)
        return rcopy(gs.at[s, yp, 0], rb.at[s, 0, 0], rs_s.at[4, s], rs_r.at[4, s], gp, i)

    def b2_m(c):
        s = slot(c)
        return rcopy(gs.at[s, ym, 1], rb.at[s, 1, 1], rs_s.at[5, s], rs_r.at[5, s], gm, i)

    def zc(c):
        s = slot(c)
        return rcopy(gs.at[s, y, oz], rz.at[s], rs_s.at[6, s], rs_r.at[6, s], gz, i)

    def e_p(c):
        s = slot(c)
        ref = hb.at[s, y, z]
        return rcopy(ref, ref, hz_s.at[0, s], hz_r.at[0, s], gp, i)

    def e_m(c):
        s = slot(c)
        ref = hb.at[s, y, z]
        return rcopy(ref, ref, hz_s.at[1, s], hz_r.at[1, s], gm, i)

    def f_p(c):
        s = slot(c)
        ref = hb.at[s, ym, z, pl.ds(0, 16)]
        return rcopy(ref, ref, hz_s.at[2, s], hz_r.at[2, s], gp, i)

    def f_m(c):
        s = slot(c)
        ref = hb.at[s, yp, z, pl.ds(16, 16)]
        return rcopy(ref, ref, hz_s.at[3, s], hz_r.at[3, s], gm, i)

    def ez(c, block, n):
        s = slot(c)
        ref = hb.at[s, block, z]
        return rcopy(ref, ref, hz_s.at[4 + n, s], hz_r.at[4 + n, s], gz, i)

    def wait_grp_sends(c):
        for copy in (a_p, a_m, b1_p, b1_m, b2_p, b2_m, zc, e_p, e_m, f_p, f_m):
            copy(c).wait_send()
        for n, block in enumerate((y, ym, yp, yd)):
            ez(c, block, n).wait_send()

    def stage_g(c):
        s = slot(c)
        rows = xb.at[c].reshape(MC, KB)
        for k in range(2):
            @pl.loop(0, 7)
            def _(n):
                cols = pl.ds(pl.multiple_of(n * 256, 256), 256)
                out = jnp.dot(rows[...], w[k, :, cols], preferred_element_type=f32)
                gs[s, :, :, :, pl.ds(pl.multiple_of(k * FB + n * 256, 256), 256)] = (
                    out.astype(bf16).reshape(4, 2, HR, 256)
                )
        a_p(c).start()
        a_m(c).start()
        b1_p(c).start()
        b1_m(c).start()

    def stage_r1(c):
        s = slot(c)
        a_p(c).wait_recv()
        gs[s, yp, 0] = (gs[s, yp, 0].astype(f32) + ra[s, 0].astype(f32)).astype(bf16)
        b2_p(c).start()
        a_m(c).wait_recv()
        gs[s, ym, 1] = (gs[s, ym, 1].astype(f32) + ra[s, 1].astype(f32)).astype(bf16)
        b2_m(c).start()

    def stage_r2(c):
        s = slot(c)
        for copy in (b1_p, b1_m, b2_p, b2_m):
            copy(c).wait_recv()
        gs[s, y, oz] = (
            gs[s, y, oz].astype(f32) + rb[s, 0, oz].astype(f32) + rb[s, 1, oz].astype(f32)
        ).astype(bf16)
        zc(c).start()

    def stage_r3(c):
        s = slot(c)
        zc(c).wait_recv()

        def part(cols):
            return (
                gs[s, y, z, :, cols].astype(f32) + rb[s, 0, z, :, cols].astype(f32)
                + rb[s, 1, z, :, cols].astype(f32) + rz[s, :, cols].astype(f32)
            )

        scale = jnp.concatenate([inv[0, c][:, 0:1], inv[1, c][:, 0:1]], axis=0)
        for n in range(7):
            gate = part(pl.ds(n * 256, 256)) * scale
            up = part(pl.ds(FB + n * 256, 256)) * scale
            hb[s, y, z, :, pl.ds(n * 256, 256)] = (gate / (1.0 + jnp.exp(-gate)) * up).astype(bf16)
        e_p(c).start()
        e_m(c).start()
        ez(c, y, 0).start()

    def stage_r4(c):
        e_p(c).wait_recv()
        f_p(c).start()
        ez(c, ym, 1).start()
        e_m(c).wait_recv()
        f_m(c).start()
        ez(c, yp, 2).start()

    def stage_r5(c):
        f_p(c).wait_recv()
        f_m(c).wait_recv()
        ez(c, yd, 3).start()

    def cc(c):
        s = lax.rem(c, 2)
        return rcopy(ps.at[s, 1 - core], rc.at[c], c_s.at[s], c_r.at[c], g, icore)

    def xc(c, d):
        s = lax.rem(c, 2)
        return rcopy(
            px.at[s, (x + d) % 4], rx.at[c, d - 1], x_s.at[d - 1, s], x_r.at[d - 1, c],
            g, (i + 4 * d) % 16,
        )

    def zhc(c):
        s = lax.rem(c, 2)
        return rcopy(pz.at[s], rzh.at[c], zh_s.at[s], zh_r.at[c], g, izh)

    def stage_dn(c):
        s, s2 = slot(c), lax.rem(c, 2)
        for n, block in enumerate((y, ym, yp, yd)):
            ez(c, block, n).wait_recv()
        rows = hb.at[s].reshape(MC, FB)

        @pl.loop(0, 4)
        def _(n):
            cols = pl.ds(pl.multiple_of(n * 256, 256), 256)
            out = jnp.dot(rows[...], wd[:, cols], preferred_element_type=f32)
            ps[s2, :, :, cols] = out.astype(bf16).reshape(2, 128, 256)

        cc(c).start()

    def stage_u1(c):
        s2 = lax.rem(c, 2)
        cc(c).wait_recv()
        px[s2] = (ps[s2, core].astype(f32) + rc[c].astype(f32)).astype(bf16).reshape(4, 2, 16, KB)
        for d in (2, 1, 3):
            xc(c, d).start()
        cc(c).wait_send()

    def sum_x(c, half):
        s2 = lax.rem(c, 2)
        out = px[s2, x, half].astype(f32)
        for d in range(3):
            out = out + rx[c, d, half].astype(f32)
        return out

    def stage_u2(c):
        for d in (1, 3, 2):
            xc(c, d).wait_recv()
        pz[lax.rem(c, 2)] = sum_x(c, 1 - zh).astype(bf16)
        zhc(c).start()

    def far_copy(c, h):
        return rcopy(th.at[c, h], tgt.at[c, core], p_s.at[h], p_r.at[c], q, 2 * g + h)

    def far(c, h, begin):
        own = me_far & (core == h)

        @pl.when(jnp.logical_not(own))
        def _():
            if begin:
                far_copy(c, h).start()
            else:
                far_copy(c, h).wait_send()

        if begin:
            @pl.when(own)
            def _():
                pltpu.make_async_copy(th.at[c, h], tgt.at[c, core], p_r.at[c]).start()

    def stage_u3(c):
        zhc(c).wait_recv()
        out = (sum_x(c, zh) + rzh[c].astype(f32)).astype(bf16)
        teach_ref[c] = out
        th[c, 0] = out[:, :SC]
        th[c, 1] = out[:, SC:]

        for h in range(2):
            far(c, h, True)
        for d in (1, 2, 3):
            xc(c, d).wait_send()
        zhc(c).wait_send()

    def py(c, d):
        ref = pg.at[c, g]
        s2 = lax.rem(c, 2)
        return rcopy(
            ref, ref, py_s.at[d - 1, s2], py_r.at[d - 1, c], z * 4 + (y + d) % 4, i
        )

    def pzc(c, d):
        ref = pg.at[c, z * 4 + (y + 4 - d) % 4]
        return rcopy(ref, ref, pz_s.at[d, lax.rem(c, 2)], pz_r.at[d, c], gz, i)

    def predict():
        load_proj.wait()
        pred[...] = jnp.tanh(
            jnp.dot(sin[...], proj[...], preferred_element_type=f32)
        ).reshape(2, C, 16, SC)

    def stage_v1(c):
        pltpu.make_async_copy(tgt.at[c], tgt.at[c], p_r.at[c]).wait()
        predicted = pred[:, c]
        mismatch = predicted - tgt[c].astype(f32)
        pg[c, g] = (mismatch * (1.0 - predicted * predicted)).astype(bf16)
        for d in (2, 1, 3):
            py(c, d).start()
        pzc(c, 0).start()
        for h in range(2):
            far(c, h, False)

    def stage_v2(c):
        for d in (1, 3, 2):
            py(c, d).wait_recv()
            pzc(c, d).start()

    def stage_v3(c):
        for d in range(4):
            pzc(c, d).wait_recv()
        rows = jnp.concatenate([sall[0, c], sall[1, c]], axis=0)
        pre = jnp.concatenate(
            [pg[c, :, 0].reshape(128, SC), pg[c, :, 1].reshape(128, SC)], axis=0
        )
        for n in range(4):
            cols = slice(n * 256, n * 256 + 256)
            gproj[cols, :] += lax.dot_general(
                rows[:, cols], pre, (((0,), (0,)), ((), ())), preferred_element_type=f32
            )
        for d in range(1, 4):
            py(c, d).wait_send()
        for d in range(4):
            pzc(c, d).wait_send()

    def a_copy(m, d):
        to = (i + d) % 16
        return rcopy(it.at[m, to // 2, to % 2], rr.at[m, 15 - d], a_s.at[d - 1], a_r.at[m], g, to)

    def b_copy(m, d):
        ref = rf.at[m, q, core]
        return rcopy(ref, ref, b_s.at[d - 1], b_r.at[m], g, (i + d) % 16)

    def each(copy, m, what):
        def body(d, _):
            what(copy(m, d))
            return 0
        lax.fori_loop(1, 16, body, 0)

    def stage_a1(m):
        own = pg[pl.ds(2 * m, 2), g].reshape(64, SC)
        for n in range(8):
            out = lax.dot_general(
                own, proj[n * 128:n * 128 + 128, :], (((1,), (1,)), ((), ())),
                preferred_element_type=f32,
            ).astype(bf16).reshape(2, 2, 16, 128)
            for b in range(2):
                it[m, n, b] = out[:, b]
        each(a_copy, m, lambda copy: copy.start())

    def stage_a2(m):
        pltpu.make_async_copy(rr.at[m], rr.at[m], a_r.at[m]).wait()
        out = it[m, q, core].astype(f32)
        for d in range(15):
            out = out + rr[m, d].astype(f32)
        rf[m, q, core] = out.astype(bf16)
        each(b_copy, m, lambda copy: copy.start())
        each(a_copy, m, lambda copy: copy.wait_send())

    def stage_a3(m):
        part = rr.at[m]
        pltpu.make_async_copy(part, part, b_r.at[m]).wait()
        for n in range(8):
            for b in range(2):
                gstu_ref[b, pl.ds(2 * m, 2), :, n * 128:n * 128 + 128] = rf[m, n, b]
        each(b_copy, m, lambda copy: copy.wait_send())

    gproj[...] = jnp.zeros_like(gproj)

    def tick(t, _):
        def run(stage, back):
            c = t - back

            @pl.when((c >= 0) & (c < C))
            def _():
                stage(c)

        def run_pair(stage, back):
            c = t - back

            @pl.when((c >= 0) & (c < C) & (c % 2 == 1))
            def _():
                stage(c // 2)

        run(wait_grp_sends, NS)
        for k in range(4):
            @pl.when(t == GROUPS[k][0])
            def _():
                t3(k).wait_recv()
        run(stage_g, 0)
        run(stage_r2, 1)
        run(stage_r4, 2)

        @pl.when(t == 3)
        def _():
            load_wd.wait()

        run(stage_dn, 3)
        run(stage_u2, 4)
        run(stage_v1, 5)
        run_pair(stage_a2, 6)

        @pl.when(t == 6)
        def _():
            t3(FAR).wait_recv()

        run(stage_v3, 6)
        run(stage_r1, 0)

        @pl.when(t == 0)
        def _():
            start_t3(1)
            scale_columns()

        run(stage_r3, 1)
        run(stage_r5, 2)
        run(stage_u1, 3)
        run(stage_u3, 4)
        run_pair(stage_a1, 5)
        run(stage_v2, 5)
        run_pair(stage_a3, 6)

        @pl.when(t == 1)
        def _():
            start_t3(2)
            pltpu.make_async_copy(
                sall.at[core, q, pl.ds(0, 112)], sall.at[core, q, pl.ds(0, 112)], s1_r
            ).wait()
            t1(FAR).start()

        @pl.when(t == 2)
        def _():
            start_t3(3)
            start_t2(FAR)
            predict()

        @pl.when(t == 4)
        def _():
            start_t3(FAR)
        return 0

    lax.fori_loop(0, C + 6, tick, 0)
    gproj_ref[...] = gproj[...].astype(bf16)

    for d in range(1, 8):
        ssq_copy(d).wait_send()
        s1_copy(d).wait_send()
    for d in range(1, 8):
        t0(d).wait_send()
    for k in range(1, 5):
        t1(k).wait_send()
        for d in range(1, 4):
            t2(k, d).wait_send()
    for k in range(5):
        t3(k).wait_send()

    @pl.when(teller)
    def _():
        for d in range(1, 16):
            inv_copy(d).wait_send()


def widen(a_ref, b_ref, c_ref, a_out, b_out, c_out):
    a_out[...] = a_ref[...]
    b_out[...] = b_ref[...].astype(f32)
    c_out[...] = c_ref[...].astype(f32)


def shards(tokens, norm_gain, gate_up_weight, down_weight, student_in, student_proj):
    vmem = pl.BlockSpec(memory_space=pltpu.VMEM)
    hbm = pl.BlockSpec(memory_space=pl.ANY)
    dma = pltpu.SemaphoreType.DMA
    teacher, grad_student, grad_proj = pl.pallas_call(
        kernel,
        out_shape=(
            jax.ShapeDtypeStruct((C, 16, KB), bf16),
            jax.ShapeDtypeStruct((2, C, 16, SD), bf16),
            jax.ShapeDtypeStruct((SD, SC), bf16),
        ),
        in_specs=[vmem, vmem, hbm, hbm, hbm, hbm],
        out_specs=(vmem, vmem, vmem),
        scratch_shapes=[
            pltpu.VMEM((2, KB, FB), bf16),
            pltpu.VMEM((FB, KB), bf16),
            pltpu.VMEM((SD, SC), bf16),
            pltpu.VMEM((256, SD), bf16),
            pltpu.VMEM((2, C, 16, SC), f32),
            pltpu.VMEM((C, 2, 8, 16, KB), bf16),
            pltpu.VMEM((2, 8, 128, SD), bf16),
            pltpu.VMEM((8, 128), f32),
            pltpu.VMEM((7, 8, 128), f32),
            pltpu.VMEM((8, 128), f32),
            pltpu.VMEM((2, 8, 128), f32),
            pltpu.VMEM((2, C, 16, 128), f32),
            pltpu.VMEM((NS, 4, 2, HR, F2), bf16),
            pltpu.VMEM((NS, 2, HR, F2), bf16),
            pltpu.VMEM((NS, 2, 2, HR, F2), bf16),
            pltpu.VMEM((NS, HR, F2), bf16),
            pltpu.VMEM((NS, 4, 2, HR, FB), bf16),
            pltpu.VMEM((2, 2, 128, KB), bf16),
            pltpu.VMEM((C, 128, KB), bf16),
            pltpu.VMEM((2, 4, 2, 16, KB), bf16),
            pltpu.VMEM((C, 3, 2, 16, KB), bf16),
            pltpu.VMEM((2, 16, KB), bf16),
            pltpu.VMEM((C, 16, KB), bf16),
            pltpu.VMEM((C, 2, 16, SC), bf16),
            pltpu.VMEM((C, 2, 16, SC), bf16),
            pltpu.VMEM((C, 8, 2, 16, SC), bf16),
            pltpu.VMEM((SD, SC), f32),
            pltpu.VMEM((4, 8, 2, 2, 16, 128), bf16),
            pltpu.VMEM((4, 15, 2, 16, 128), bf16),
            pltpu.VMEM((4, 8, 2, 2, 16, 128), bf16),
            dma((4,)),
            dma((7,)), dma(()),
            dma((15,)), dma((2,)),
            dma((7,)), dma(()),
            dma((7,)), dma((7,)),
            dma((5,)), dma((5,)),
            dma((5, 3)), dma((5, 3)),
            dma((5,)), dma((5,)),
            dma((7, NS)), dma((7, NS)),
            dma((8, NS)), dma((8, NS)),
            dma((2,)), dma((C,)),
            dma((3, 2)), dma((3, C)),
            dma((2,)), dma((C,)),
            dma((2,)), dma((C,)),
            dma((3, 2)), dma((3, C)),
            dma((4, 2)), dma((4, C)),
            dma((15,)), dma((4,)),
            dma((15,)), dma((4,)),
        ],
        compiler_params=pltpu.CompilerParams(
            collective_id=0, has_side_effects=True, vmem_limit_bytes=62 * 1024 * 1024
        ),
    )(tokens, norm_gain, gate_up_weight, down_weight, student_in, student_proj)
    return pl.pallas_call(
        widen,
        grid=(4,),
        out_shape=(
            jax.ShapeDtypeStruct((128, KB), bf16),
            jax.ShapeDtypeStruct((256, SD), f32),
            jax.ShapeDtypeStruct((SD, SC), f32),
        ),
        in_specs=[
            pl.BlockSpec((32, KB), lambda n: (n, 0)),
            pl.BlockSpec((64, SD), lambda n: (n, 0)),
            pl.BlockSpec((256, SC), lambda n: (n, 0)),
        ],
        out_specs=(
            pl.BlockSpec((32, KB), lambda n: (n, 0)),
            pl.BlockSpec((64, SD), lambda n: (n, 0)),
            pl.BlockSpec((256, SC), lambda n: (n, 0)),
        ),
    )(teacher.reshape(128, KB), grad_student.reshape(256, SD), grad_proj)


def solution(mesh):
    return jax.shard_map(
        shards,
        mesh=mesh,
        in_specs=(
            P("inner", "grp"),
            P("grp"),
            P(None, "grp", "inner"),
            P("inner", "grp"),
            P("grp", None),
            P(None, "inner"),
        ),
        out_specs=(P("inner", "grp"), P("grp", None), P(None, "inner")),
        check_vma=False,
    )
```

```python
import jax
import jax.numpy as jnp
from jax import lax
from jax.experimental import pallas as pl
from jax.experimental.pallas import tpu as pltpu
from jax.sharding import PartitionSpec as P

D = 8192
KB = 1024
FB = 1792
F2 = 2 * FB
SD = 1024
SC = 512
C = 8
MC = 256
HR = 32
NS = 4
GROUPS = ((0, 1), (1, 1), (2, 2), (4, 4))
FAR = 4
f32, bf16 = jnp.float32, jnp.bfloat16
MESH = pl.DeviceIdType.MESH


def kernel(
    tok_ref, gain_ref, w_hbm, wd_hbm, sin_hbm, proj_hbm,
    teach_ref, gstu_ref, gproj_ref,
    w, wd, proj, sin, pred, xb, sall, ssq, ssqr, inv_own, inv_line, inv,
    gs, ra, rb, rz, hb, ps, rc, px, rx, pz, rzh, th, tgt, pg, gproj, it, rr, rf,
    lsem, ssq_s, ssq_r, inv_s, inv_r, s1_s, s1_r, t0_s, t0_r, t1_s, t1_r, t2_s, t2_r, t3_s, t3_r,
    rs_s, rs_r, hz_s, hz_r, c_s, c_r, x_s, x_r, zh_s, zh_r, p_s, p_r,
    py_s, py_r, pz_s, pz_r, a_s, a_r, b_s, b_r,
):
    g = lax.axis_index("grp")
    i = lax.axis_index("inner")
    z, y = g // 4, g % 4
    x, core, q = i // 4, i % 2, i // 2
    yp, ym, yd = (y + 1) % 4, (y + 3) % 4, (y + 2) % 4
    gp, gm = z * 4 + yp, z * 4 + ym
    gz = (1 - z) * 4 + y
    oz = 1 - z
    zh = q % 2
    izh = x * 4 + (1 - zh) * 2 + core
    icore = x * 4 + zh * 2 + (1 - core)
    pos = core * 8 + q
    me_far = g == q

    def rcopy(src, dst, ss, rs, dg, di):
        return pltpu.make_async_remote_copy(
            src_ref=src, dst_ref=dst, send_sem=ss, recv_sem=rs,
            device_id=(dg, di), device_id_type=MESH,
        )

    load_w = pltpu.make_async_copy(w_hbm, w, lsem.at[0])
    load_wd = pltpu.make_async_copy(wd_hbm, wd, lsem.at[1])
    load_proj = pltpu.make_async_copy(proj_hbm, proj, lsem.at[2])
    rows16 = pl.ds(pl.multiple_of(pos * 16, 16), 16)
    my16 = pl.ds(pl.multiple_of(g * 16, 16), 16)
    load_sin = pltpu.make_async_copy(sin_hbm, sin, lsem.at[3])
    load_w.start()
    load_wd.start()
    load_proj.start()
    load_sin.start()

    barrier = pltpu.get_barrier_semaphore()

    def greet_grp(d, _):
        pl.semaphore_signal(barrier, inc=1, device_id=((g + d) % 8, i), device_id_type=MESH)
        return 0

    def greet_inner(d, _):
        pl.semaphore_signal(barrier, inc=1, device_id=(g, (i + d) % 16), device_id_type=MESH)
        return 0

    lax.fori_loop(1, 8, greet_grp, 0)
    lax.fori_loop(1, 16, greet_inner, 0)
    for h in range(2):
        @pl.when(jnp.logical_not(me_far & (core == h)))
        def _():
            pl.semaphore_signal(barrier, inc=1, device_id=(q, 2 * g + h), device_id_type=MESH)

    values = tok_ref[...].astype(f32)
    total = jnp.sum(values * values, axis=1, keepdims=True)
    ssq[...] = jnp.broadcast_to(total, (128, 128)).T[0:8]

    xb[:, core, q] = (values * gain_ref[...].astype(f32).reshape(1, KB)).astype(bf16).reshape(8, 16, KB)
    pl.semaphore_wait(barrier, jnp.where(me_far, 23, 24))

    def ssq_copy(d):
        return rcopy(ssq, ssqr.at[7 - d], ssq_s.at[d - 1], ssq_r, (g + d) % 8, i)

    def s1_copy(d):
        return rcopy(
            sin.at[rows16], sall.at[core, q, my16], s1_s.at[d - 1], s1_r, (g + d) % 8, i
        )

    teller = g == ((q // 2) % 2) * 4 + core * 2 + q // 4

    def inv_copy(d):
        return rcopy(inv_own, inv_line.at[q % 2], inv_s.at[d - 1], inv_r.at[q % 2], g, (i + d) % 16)

    def scales():
        pltpu.make_async_copy(ssqr, ssqr, ssq_r).wait()
        line = ssq[...]
        for d in range(7):
            line = line + ssqr[d]
        inv_own[...] = lax.rsqrt(line / D + 1e-05)

        @pl.when(teller)
        def _():
            for d in range(1, 16):
                inv_copy(d).start()

    def scale_columns():
        for k in range(2):
            mine = teller & (q % 2 == k)

            @pl.when(mine)
            def _():
                inv_line[k] = inv_own[...]

            @pl.when(jnp.logical_not(mine))
            def _():
                pltpu.make_async_copy(inv_line.at[k], inv_line.at[k], inv_r.at[k]).wait()

            inv[k] = jnp.broadcast_to(inv_line[k, 0:1], (128, 128)).T.reshape(C, 16, 128)

    x2 = pl.ds(pl.multiple_of(x * 2, 2), 2)

    def t0(d):
        ref = xb.at[0, core, q]
        return rcopy(ref, ref, t0_s.at[d - 1], t0_r.at[d - 1], g, (i + 2 * d) % 16)

    def t1(k):
        if k == FAR:
            ref = sall.at[core, q]
        else:
            ref = xb.at[pl.ds(GROUPS[k][0], GROUPS[k][1]), core, q]
        return rcopy(ref, ref, t1_s.at[k], t1_r.at[k], g, izh)

    def t2(k, d):
        if k == FAR:
            ref = sall.at[core, x2]
        else:
            ref = xb.at[pl.ds(GROUPS[k][0], GROUPS[k][1]), core, x2]
        return rcopy(ref, ref, t2_s.at[k, d - 1], t2_r.at[k, d - 1], g, (i + 4 * d) % 16)

    def t3(k):
        if k == FAR:
            ref = sall.at[core]
        else:
            ref = xb.at[pl.ds(GROUPS[k][0], GROUPS[k][1]), core]
        return rcopy(ref, ref, t3_s.at[k], t3_r.at[k], g, icore)

    def start_t2(k):
        t1(k).wait_recv()
        for d in (2, 1, 3):
            t2(k, d).start()

    def start_t3(k):
        for d in (1, 3, 2):
            t2(k, d).wait_recv()
        t3(k).start()

    for d in (4, 3, 5, 2, 6, 1, 7):
        t0(d).start()
    for k in range(1, 4):
        t1(k).start()
    for d in range(1, 8):
        ssq_copy(d).start()
    for d in range(1, 8):
        t0(d).wait_recv()
    t3(0).start()
    scales()
    for k in range(1, 4):
        start_t2(k)
    load_sin.wait()
    sall[core, q, my16] = sin[rows16]
    for d in range(1, 8):
        s1_copy(d).start()
    load_w.wait()

    def slot(c):
        return lax.rem(c, NS)

    def a_p(c):
        s = slot(c)
        return rcopy(gs.at[s, yd, 0], ra.at[s, 0], rs_s.at[0, s], rs_r.at[0, s], gp, i)

    def a_m(c):
        s = slot(c)
        return rcopy(gs.at[s, yd, 1], ra.at[s, 1], rs_s.at[1, s], rs_r.at[1, s], gm, i)

    def b1_p(c):
        s = slot(c)
        return rcopy(gs.at[s, yp, 1], rb.at[s, 0, 1], rs_s.at[2, s], rs_r.at[2, s], gp, i)

    def b1_m(c):
        s = slot(c)
        return rcopy(gs.at[s, ym, 0], rb.at[s, 1, 0], rs_s.at[3, s], rs_r.at[3, s], gm, i)

    def b2_p(c):
        s = slot(c)
        return rcopy(gs.at[s, yp, 0], rb.at[s, 0, 0], rs_s.at[4, s], rs_r.at[4, s], gp, i)

    def b2_m(c):
        s = slot(c)
        return rcopy(gs.at[s, ym, 1], rb.at[s, 1, 1], rs_s.at[5, s], rs_r.at[5, s], gm, i)

    def zc(c):
        s = slot(c)
        return rcopy(gs.at[s, y, oz], rz.at[s], rs_s.at[6, s], rs_r.at[6, s], gz, i)

    def e_p(c):
        s = slot(c)
        ref = hb.at[s, y, z]
        return rcopy(ref, ref, hz_s.at[0, s], hz_r.at[0, s], gp, i)

    def e_m(c):
        s = slot(c)
        ref = hb.at[s, y, z]
        return rcopy(ref, ref, hz_s.at[1, s], hz_r.at[1, s], gm, i)

    def f_p(c):
        s = slot(c)
        ref = hb.at[s, ym, z, pl.ds(0, 16)]
        return rcopy(ref, ref, hz_s.at[2, s], hz_r.at[2, s], gp, i)

    def f_m(c):
        s = slot(c)
        ref = hb.at[s, yp, z, pl.ds(16, 16)]
        return rcopy(ref, ref, hz_s.at[3, s], hz_r.at[3, s], gm, i)

    def ez(c, block, n):
        s = slot(c)
        ref = hb.at[s, block, z]
        return rcopy(ref, ref, hz_s.at[4 + n, s], hz_r.at[4 + n, s], gz, i)

    def wait_grp_sends(c):
        for copy in (a_p, a_m, b1_p, b1_m, b2_p, b2_m, zc, e_p, e_m, f_p, f_m):
            copy(c).wait_send()
        for n, block in enumerate((y, ym, yp, yd)):
            ez(c, block, n).wait_send()

    def stage_g(c):
        s = slot(c)
        rows = xb.at[c].reshape(MC, KB)
        for k in range(2):
            @pl.loop(0, 2)
            def _(n):
                cols = pl.ds(pl.multiple_of(n * 896, 128), 896)
                out = jnp.dot(rows[...], w[k, :, cols], preferred_element_type=f32)
                gs[s, :, :, :, pl.ds(pl.multiple_of(k * FB + n * 896, 128), 896)] = (
                    out.astype(bf16).reshape(4, 2, HR, 896)
                )
        a_p(c).start()
        a_m(c).start()

    def stage_b1(c):
        b1_p(c).start()
        b1_m(c).start()

    def stage_r1(c):
        s = slot(c)
        a_p(c).wait_recv()
        gs[s, yp, 0] = (gs[s, yp, 0].astype(f32) + ra[s, 0].astype(f32)).astype(bf16)
        b2_p(c).start()
        a_m(c).wait_recv()
        gs[s, ym, 1] = (gs[s, ym, 1].astype(f32) + ra[s, 1].astype(f32)).astype(bf16)
        b2_m(c).start()

    def stage_r2(c):
        s = slot(c)
        for copy in (b1_p, b1_m, b2_p, b2_m):
            copy(c).wait_recv()
        gs[s, y, oz] = (
            gs[s, y, oz].astype(f32) + rb[s, 0, oz].astype(f32) + rb[s, 1, oz].astype(f32)
        ).astype(bf16)
        zc(c).start()

    def stage_r3(c):
        s = slot(c)
        zc(c).wait_recv()

        def part(cols):
            return (
                gs[s, y, z, :, cols].astype(f32) + rb[s, 0, z, :, cols].astype(f32)
                + rb[s, 1, z, :, cols].astype(f32) + rz[s, :, cols].astype(f32)
            )

        scale = jnp.concatenate([inv[0, c][:, 0:1], inv[1, c][:, 0:1]], axis=0)
        for n in range(7):
            gate = part(pl.ds(n * 256, 256)) * scale
            up = part(pl.ds(FB + n * 256, 256)) * scale
            hb[s, y, z, :, pl.ds(n * 256, 256)] = (gate / (1.0 + jnp.exp(-gate)) * up).astype(bf16)
        e_p(c).start()
        e_m(c).start()
        ez(c, y, 0).start()

    def stage_r4(c):
        e_p(c).wait_recv()
        f_p(c).start()
        e_m(c).wait_recv()
        f_m(c).start()
        ez(c, ym, 1).start()
        ez(c, yp, 2).start()

    def stage_r5(c):
        f_p(c).wait_recv()
        f_m(c).wait_recv()
        ez(c, yd, 3).start()

    def cc(c):
        s = lax.rem(c, 2)
        return rcopy(ps.at[s, 1 - core], rc.at[c], c_s.at[s], c_r.at[c], g, icore)

    def xc(c, d):
        s = lax.rem(c, 2)
        return rcopy(
            px.at[s, (x + d) % 4], rx.at[c, d - 1], x_s.at[d - 1, s], x_r.at[d - 1, c],
            g, (i + 4 * d) % 16,
        )

    def zhc(c):
        s = lax.rem(c, 2)
        return rcopy(pz.at[s], rzh.at[c], zh_s.at[s], zh_r.at[c], g, izh)

    def stage_dn(c):
        s, s2 = slot(c), lax.rem(c, 2)
        for n, block in enumerate((y, ym, yp, yd)):
            ez(c, block, n).wait_recv()
        rows = hb.at[s].reshape(MC, FB)

        @pl.loop(0, 4)
        def _(n):
            cols = pl.ds(pl.multiple_of(n * 256, 256), 256)
            out = jnp.dot(rows[...], wd[:, cols], preferred_element_type=f32)
            ps[s2, :, :, cols] = out.astype(bf16).reshape(2, 128, 256)

        cc(c).start()

    def stage_u1(c):
        s2 = lax.rem(c, 2)
        cc(c).wait_recv()
        px[s2] = (ps[s2, core].astype(f32) + rc[c].astype(f32)).astype(bf16).reshape(4, 2, 16, KB)
        for d in (2, 1, 3):
            xc(c, d).start()
        cc(c).wait_send()

    def sum_x(c, half):
        s2 = lax.rem(c, 2)
        out = px[s2, x, half].astype(f32)
        for d in range(3):
            out = out + rx[c, d, half].astype(f32)
        return out

    def stage_u2(c):
        for d in (1, 3, 2):
            xc(c, d).wait_recv()
        pz[lax.rem(c, 2)] = sum_x(c, 1 - zh).astype(bf16)
        zhc(c).start()

    def far_copy(c, h):
        return rcopy(th.at[c, h], tgt.at[c, core], p_s.at[h], p_r.at[c], q, 2 * g + h)

    def far(c, h, begin):
        own = me_far & (core == h)

        @pl.when(jnp.logical_not(own))
        def _():
            if begin:
                far_copy(c, h).start()
            else:
                far_copy(c, h).wait_send()

        if begin:
            @pl.when(own)
            def _():
                pltpu.make_async_copy(th.at[c, h], tgt.at[c, core], p_r.at[c]).start()

    def stage_u3(c):
        zhc(c).wait_recv()
        out = (sum_x(c, zh) + rzh[c].astype(f32)).astype(bf16)
        teach_ref[c] = out
        th[c, 0] = out[:, :SC]
        th[c, 1] = out[:, SC:]

        for h in range(2):
            far(c, h, True)
        for d in (1, 2, 3):
            xc(c, d).wait_send()
        zhc(c).wait_send()

    def py(c, d):
        ref = pg.at[c, g]
        s2 = lax.rem(c, 2)
        return rcopy(
            ref, ref, py_s.at[d - 1, s2], py_r.at[d - 1, c], z * 4 + (y + d) % 4, i
        )

    def pzc(c, d):
        ref = pg.at[c, z * 4 + (y + 4 - d) % 4]
        return rcopy(ref, ref, pz_s.at[d, lax.rem(c, 2)], pz_r.at[d, c], gz, i)

    def predict():
        load_proj.wait()
        pred[...] = jnp.tanh(
            jnp.dot(sin[...], proj[...], preferred_element_type=f32)
        ).reshape(2, C, 16, SC)

    def stage_v1(c):
        pltpu.make_async_copy(tgt.at[c], tgt.at[c], p_r.at[c]).wait()
        predicted = pred[:, c]
        mismatch = predicted - tgt[c].astype(f32)
        pg[c, g] = (mismatch * (1.0 - predicted * predicted)).astype(bf16)
        for d in (2, 1, 3):
            py(c, d).start()
        pzc(c, 0).start()
        for h in range(2):
            far(c, h, False)

    def stage_v2(c):
        for d in (1, 3, 2):
            py(c, d).wait_recv()
            pzc(c, d).start()

    def stage_v3(c):
        for d in range(4):
            pzc(c, d).wait_recv()
        rows = jnp.concatenate([sall[0, c], sall[1, c]], axis=0)
        pre = jnp.concatenate(
            [pg[c, :, 0].reshape(128, SC), pg[c, :, 1].reshape(128, SC)], axis=0
        )
        for n in range(4):
            cols = slice(n * 256, n * 256 + 256)
            gproj[cols, :] += lax.dot_general(
                rows[:, cols], pre, (((0,), (0,)), ((), ())), preferred_element_type=f32
            )
        for d in range(1, 4):
            py(c, d).wait_send()
        for d in range(4):
            pzc(c, d).wait_send()

    def a_copy(m, d):
        to = (i + d) % 16
        return rcopy(it.at[m, to // 2, to % 2], rr.at[m, 15 - d], a_s.at[d - 1], a_r.at[m], g, to)

    def b_copy(m, d):
        ref = rf.at[m, q, core]
        return rcopy(ref, ref, b_s.at[d - 1], b_r.at[m], g, (i + d) % 16)

    def each(copy, m, what):
        def body(d, _):
            what(copy(m, d))
            return 0
        lax.fori_loop(1, 16, body, 0)

    def stage_a1(m):
        own = pg[pl.ds(2 * m, 2), g].reshape(64, SC)
        for n in range(8):
            out = lax.dot_general(
                own, proj[n * 128:n * 128 + 128, :], (((1,), (1,)), ((), ())),
                preferred_element_type=f32,
            ).astype(bf16).reshape(2, 2, 16, 128)
            for b in range(2):
                it[m, n, b] = out[:, b]
        each(a_copy, m, lambda copy: copy.start())

    def stage_a2(m):
        pltpu.make_async_copy(rr.at[m], rr.at[m], a_r.at[m]).wait()
        out = it[m, q, core].astype(f32)
        for d in range(15):
            out = out + rr[m, d].astype(f32)
        rf[m, q, core] = out.astype(bf16)
        each(b_copy, m, lambda copy: copy.start())
        each(a_copy, m, lambda copy: copy.wait_send())

    def stage_a3(m):
        part = rr.at[m]
        pltpu.make_async_copy(part, part, b_r.at[m]).wait()
        for n in range(8):
            for b in range(2):
                gstu_ref[b, pl.ds(2 * m, 2), :, n * 128:n * 128 + 128] = rf[m, n, b]
        each(b_copy, m, lambda copy: copy.wait_send())

    gproj[...] = jnp.zeros_like(gproj)

    def tick(t, _):
        def run(stage, back):
            c = t - back

            @pl.when((c >= 0) & (c < C))
            def _():
                stage(c)

        def run_pair(stage, back):
            c = t - back

            @pl.when((c >= 0) & (c < C) & (c % 2 == 1))
            def _():
                stage(c // 2)

        run(wait_grp_sends, NS)
        for k in range(4):
            @pl.when(t == GROUPS[k][0])
            def _():
                t3(k).wait_recv()
        run(stage_g, 0)
        run(stage_r2, 1)
        run(stage_r4, 2)
        run(stage_b1, 0)

        @pl.when(t == 3)
        def _():
            load_wd.wait()

        run(stage_dn, 3)
        run(stage_u2, 4)
        run(stage_v1, 5)
        run_pair(stage_a2, 6)

        @pl.when(t == 6)
        def _():
            t3(FAR).wait_recv()

        run(stage_v3, 6)
        run(stage_r1, 0)

        @pl.when(t == 0)
        def _():
            start_t3(1)
            scale_columns()

        run(stage_r3, 1)
        run(stage_r5, 2)
        run(stage_u1, 3)
        run(stage_u3, 4)
        run_pair(stage_a1, 5)
        run(stage_v2, 5)
        run_pair(stage_a3, 6)

        @pl.when(t == 1)
        def _():
            start_t3(2)
            pltpu.make_async_copy(
                sall.at[core, q, pl.ds(0, 112)], sall.at[core, q, pl.ds(0, 112)], s1_r
            ).wait()
            t1(FAR).start()

        @pl.when(t == 2)
        def _():
            start_t3(3)
            start_t2(FAR)
            predict()

        @pl.when(t == 4)
        def _():
            start_t3(FAR)
        return 0

    lax.fori_loop(0, C + 6, tick, 0)
    gproj_ref[...] = gproj[...].astype(bf16)

    for d in range(1, 8):
        ssq_copy(d).wait_send()
        s1_copy(d).wait_send()
    for d in range(1, 8):
        t0(d).wait_send()
    for k in range(1, 5):
        t1(k).wait_send()
        for d in range(1, 4):
            t2(k, d).wait_send()
    for k in range(5):
        t3(k).wait_send()

    @pl.when(teller)
    def _():
        for d in range(1, 16):
            inv_copy(d).wait_send()


def widen(a_ref, b_ref, c_ref, a_out, b_out, c_out):
    a_out[...] = a_ref[...]
    b_out[...] = b_ref[...].astype(f32)
    c_out[...] = c_ref[...].astype(f32)


def shards(tokens, norm_gain, gate_up_weight, down_weight, student_in, student_proj):
    vmem = pl.BlockSpec(memory_space=pltpu.VMEM)
    hbm = pl.BlockSpec(memory_space=pl.ANY)
    dma = pltpu.SemaphoreType.DMA
    teacher, grad_student, grad_proj = pl.pallas_call(
        kernel,
        out_shape=(
            jax.ShapeDtypeStruct((C, 16, KB), bf16),
            jax.ShapeDtypeStruct((2, C, 16, SD), bf16),
            jax.ShapeDtypeStruct((SD, SC), bf16),
        ),
        in_specs=[vmem, vmem, hbm, hbm, hbm, hbm],
        out_specs=(vmem, vmem, vmem),
        scratch_shapes=[
            pltpu.VMEM((2, KB, FB), bf16),
            pltpu.VMEM((FB, KB), bf16),
            pltpu.VMEM((SD, SC), bf16),
            pltpu.VMEM((256, SD), bf16),
            pltpu.VMEM((2, C, 16, SC), f32),
            pltpu.VMEM((C, 2, 8, 16, KB), bf16),
            pltpu.VMEM((2, 8, 128, SD), bf16),
            pltpu.VMEM((8, 128), f32),
            pltpu.VMEM((7, 8, 128), f32),
            pltpu.VMEM((8, 128), f32),
            pltpu.VMEM((2, 8, 128), f32),
            pltpu.VMEM((2, C, 16, 128), f32),
            pltpu.VMEM((NS, 4, 2, HR, F2), bf16),
            pltpu.VMEM((NS, 2, HR, F2), bf16),
            pltpu.VMEM((NS, 2, 2, HR, F2), bf16),
            pltpu.VMEM((NS, HR, F2), bf16),
            pltpu.VMEM((NS, 4, 2, HR, FB), bf16),
            pltpu.VMEM((2, 2, 128, KB), bf16),
            pltpu.VMEM((C, 128, KB), bf16),
            pltpu.VMEM((2, 4, 2, 16, KB), bf16),
            pltpu.VMEM((C, 3, 2, 16, KB), bf16),
            pltpu.VMEM((2, 16, KB), bf16),
            pltpu.VMEM((C, 16, KB), bf16),
            pltpu.VMEM((C, 2, 16, SC), bf16),
            pltpu.VMEM((C, 2, 16, SC), bf16),
            pltpu.VMEM((C, 8, 2, 16, SC), bf16),
            pltpu.VMEM((SD, SC), f32),
            pltpu.VMEM((4, 8, 2, 2, 16, 128), bf16),
            pltpu.VMEM((4, 15, 2, 16, 128), bf16),
            pltpu.VMEM((4, 8, 2, 2, 16, 128), bf16),
            dma((4,)),
            dma((7,)), dma(()),
            dma((15,)), dma((2,)),
            dma((7,)), dma(()),
            dma((7,)), dma((7,)),
            dma((5,)), dma((5,)),
            dma((5, 3)), dma((5, 3)),
            dma((5,)), dma((5,)),
            dma((7, NS)), dma((7, NS)),
            dma((8, NS)), dma((8, NS)),
            dma((2,)), dma((C,)),
            dma((3, 2)), dma((3, C)),
            dma((2,)), dma((C,)),
            dma((2,)), dma((C,)),
            dma((3, 2)), dma((3, C)),
            dma((4, 2)), dma((4, C)),
            dma((15,)), dma((4,)),
            dma((15,)), dma((4,)),
        ],
        compiler_params=pltpu.CompilerParams(
            collective_id=0, has_side_effects=True, vmem_limit_bytes=62 * 1024 * 1024
        ),
    )(tokens, norm_gain, gate_up_weight, down_weight, student_in, student_proj)
    return pl.pallas_call(
        widen,
        grid=(4,),
        out_shape=(
            jax.ShapeDtypeStruct((128, KB), bf16),
            jax.ShapeDtypeStruct((256, SD), f32),
            jax.ShapeDtypeStruct((SD, SC), f32),
        ),
        in_specs=[
            pl.BlockSpec((32, KB), lambda n: (n, 0)),
            pl.BlockSpec((64, SD), lambda n: (n, 0)),
            pl.BlockSpec((256, SC), lambda n: (n, 0)),
        ],
        out_specs=(
            pl.BlockSpec((32, KB), lambda n: (n, 0)),
            pl.BlockSpec((64, SD), lambda n: (n, 0)),
            pl.BlockSpec((256, SC), lambda n: (n, 0)),
        ),
    )(teacher.reshape(128, KB), grad_student.reshape(256, SD), grad_proj)


def solution(mesh):
    return jax.shard_map(
        shards,
        mesh=mesh,
        in_specs=(
            P("inner", "grp"),
            P("grp"),
            P(None, "grp", "inner"),
            P("inner", "grp"),
            P("grp", None),
            P(None, "inner"),
        ),
        out_specs=(P("inner", "grp"), P("grp", None), P(None, "inner")),
        check_vma=False,
    )
```
